32 devices in a mesh: lat: 4 (over y, core), lon: 8 (over z, x).
Axes of the slice: x: 2, y: 2, z: 4, core: 2. Of those that a mesh axis runs over, the one named last changes fastest.
Arguments:
- features: bfloat16 [128, 64, 1024], P('lat', 'lon'), may hold values from -18 to 18
- depth_kernel: bfloat16 [7, 7, 1024], replicated, may hold values from -0.875 to 0.875
- depth_bias: float32 [1024], replicated, may hold values from -3 to 3
- norm_gain: float32 [1024], replicated, may hold values from 0.1 to 1.9
- norm_bias: float32 [1024], replicated, may hold values from -3 to 3
- up_weight: bfloat16 [1024, 4096], P('lon', 'lat'), may hold values from -0.1875 to 0.1875
- up_bias: float32 [4096], P('lat'), may hold values from -3 to 3
- down_weight: bfloat16 [1024, 4096], P('lon', 'lat'), may hold values from -0.09375 to 0.09375
- down_bias: float32 [1024], replicated, may hold values from -3 to 3
- layer_scale: float32 [1024], replicated, may hold values from 0.3 to 2
Outputs:
- updated: bfloat16 [128, 64, 1024], P('lat', 'lon')
The draws below stay inside these ranges and needn't reach their ends.
All inputs are finite; a program needn't handle non-finite values.
Results may differ from the reference program's by a relative error of at most 0.0085.
Values may be sent and summed in bfloat16 or wider, within the bound.
No kernel may reach another device: no remote copies, remote signals or barrier semaphores. Data moves between devices by JAX's collectives and lax.ppermute only.
A program may use at most 64 MiB of HBM per device.

```python
import math
import jax
import jax.numpy as jnp
from jax import lax

C = 1024
HID = 4096
HEIGHT = 128
WIDTH = 64
N_LAT = 4


def draw_features(key, part):
    first, second = jax.random.split(jax.random.fold_in(key, 17), 2)
    channel_scale = jnp.exp(jax.random.uniform(second, (C,), jnp.float32, -1.2, 1.2))
    base = jax.random.truncated_normal(first, -4.0, 4.0, (HEIGHT, WIDTH, C), jnp.float32)
    values = base * channel_scale
    return values.astype(jnp.bfloat16)


def steps_of(key, dims, pieces, least, largest):
    def one(axis_at, shards_of):
        draws = jax.random.uniform(jax.random.fold_in(jax.random.fold_in(key, 6), axis_at), (shards_of,), jnp.float32, least / len(pieces), largest / len(pieces))
        return jnp.repeat(jnp.exp(draws), dims[axis_at] // shards_of).reshape((-1,) + (1,) * (len(dims) - axis_at - 1))

    loudness = one(*pieces[0])
    for cut in pieces[1:]:
        loudness = loudness * one(*cut)
    return loudness


def centred(rng, dims, scale, bound, pieces=(), dtype=jnp.bfloat16):
    level = steps_of(rng, dims, pieces, -0.22, 0.18) if pieces else 1.0
    result = jax.random.normal(rng, dims, jnp.float32) * scale * level
    return jnp.minimum(jnp.maximum(result, -bound), bound).astype(dtype)


def setup_inputs(seed: int = 0) -> dict:
    splits = jax.random.split(jax.random.key(seed), 11)
    return {
        "features": draw_features(jax.random.fold_in(splits[10], 71), 0),
        "depth_kernel": centred(splits[1], (7, 7, C), 49 ** -0.5, 0.875),
        "depth_bias": centred(splits[2], (C,), 0.5, 3.0, (), jnp.float32),
        "norm_gain": jnp.clip(1.0 + 0.18 * jax.random.normal(splits[3], (C,), jnp.float32), 0.1, 1.9),
        "norm_bias": centred(splits[4], (C,), 0.5, 3.0, (), jnp.float32),
        "up_weight": centred(splits[5], (C, HID), C ** -0.5, 0.1875, ((0, 8), (1, 4))),
        "up_bias": centred(splits[6], (HID,), 0.5, 3.0, ((0, 4),), jnp.float32),
        "down_weight": centred(splits[7], (C, HID), HID ** -0.5, 0.09375, ((0, 8), (1, 4))),
        "down_bias": centred(splits[8], (C,), 0.5, 3.0, (), jnp.float32),
        "layer_scale": jnp.clip(jnp.exp(jax.random.uniform(splits[9], (C,), jnp.float32, math.log(0.3), math.log(2.0))), 0.3, 2.0),
    }


def depthwise_conv(features, depth_kernel, depth_bias):
    values = features.astype(jnp.float32)
    wrapped = jnp.concatenate([values[:, -3:], values, values[:, :3]], axis=1)
    padded = jnp.pad(wrapped, ((3, 3), (0, 0), (0, 0)))
    height, width = (features.shape[0], features.shape[1])
    total = jnp.zeros(values.shape, jnp.float32) + depth_bias.astype(jnp.float32)
    kernel = depth_kernel.astype(jnp.float32)
    for row_off in range(7):
        for col_off in range(7):
            total = total + padded[row_off:row_off + height, col_off:col_off + width] * kernel[row_off, col_off]
    return total

def layer_norm(values, norm_gain, norm_bias):
    centre = lax.optimization_barrier(jnp.mean(values, axis=-1, keepdims=True))
    spread = lax.optimization_barrier(jnp.mean((values - centre) ** 2, axis=-1, keepdims=True))
    return ((values - centre) * lax.rsqrt(spread + 1e-06) * norm_gain + norm_bias).astype(jnp.bfloat16)

def reference(features, depth_kernel, depth_bias, norm_gain, norm_bias, up_weight, up_bias, down_weight, down_bias, layer_scale):
    depthwise = depthwise_conv(features, depth_kernel, depth_bias)
    normed = layer_norm(depthwise, norm_gain, norm_bias)
    quarter = HID // N_LAT

    def one_row(row_pixels):
        pre = jnp.dot(row_pixels, up_weight, preferred_element_type=jnp.float32) + up_bias
        hidden = jax.nn.gelu(pre, approximate=False).astype(jnp.bfloat16)
        branch = jnp.zeros((row_pixels.shape[0], C), jnp.float32)
        for block in range(N_LAT):
            part_hidden = hidden[:, block * quarter:(block + 1) * quarter]
            part_weight = down_weight[:, block * quarter:(block + 1) * quarter]
            product = lax.dot_general(part_hidden, part_weight, (((1,), (1,)), ((), ())), preferred_element_type=jnp.float32)
            rounded = lax.optimization_barrier(product.astype(jnp.bfloat16))
            branch = branch + rounded.astype(jnp.float32)
        return branch
    branch = lax.map(one_row, normed)
    updated = features.astype(jnp.float32) + layer_scale * (branch + down_bias)
    return updated.astype(jnp.bfloat16)
```

```python
import functools

import jax
import jax.numpy as jnp
from jax import lax
from jax.experimental import pallas as pl
from jax.experimental.pallas import tpu as pltpu
from jax.sharding import PartitionSpec as P

F32 = jnp.float32
BF16 = jnp.bfloat16
LANES = 128
VMEM = pl.BlockSpec(memory_space=pltpu.VMEM)
SMEM = pl.BlockSpec(memory_space=pltpu.SMEM)
PARAMS = pltpu.CompilerParams(vmem_limit_bytes=40 * 1024 * 1024)


def shift(value, axis, step, inner):
    count = lax.axis_size(axis)
    return lax.ppermute(value, axis, [(i, (i + step * inner) % count) for i in range(count)])


def swap(value, axis, bit):
    count = lax.axis_size(axis)
    return lax.ppermute(value, axis, [(i, i ^ bit) for i in range(count)])


def edges_kernel(low_ref, mid_ref, high_ref, first_ref, last_ref, slab):
    rows, cols, chans = mid_ref.shape

    @pl.loop(0, chans // LANES)
    def _(chunk):
        lanes = pl.ds(pl.multiple_of(chunk * LANES, LANES), LANES)
        slab[pl.ds(0, 3 * cols), :] = low_ref[:, :, lanes].astype(F32).reshape(3 * cols, LANES)
        slab[pl.ds(3 * cols, rows * cols), :] = mid_ref[:, :, lanes].astype(F32).reshape(rows * cols, LANES)
        slab[pl.ds((3 + rows) * cols, 3 * cols), :] = high_ref[:, :, lanes].astype(F32).reshape(3 * cols, LANES)
        for col in range(3):
            first_ref[col, :, lanes] = slab[pl.ds(col, rows + 6, stride=cols), :].astype(BF16)
            last_ref[col, :, lanes] = slab[pl.ds(cols - 3 + col, rows + 6, stride=cols), :].astype(BF16)


def edges(low, mid, high):
    rows, cols, chans = mid.shape
    shape = jax.ShapeDtypeStruct((3, rows + 6, chans), BF16)
    return pl.pallas_call(
        edges_kernel,
        out_shape=(shape, shape),
        in_specs=[VMEM] * 3,
        out_specs=(VMEM, VMEM),
        scratch_shapes=[pltpu.VMEM(((rows + 6) * cols, LANES), F32)],
        compiler_params=PARAMS,
    )(low, mid, high)


def conv_kernel(
    order_ref, mid_ref, low_ref, high_ref, left_ref, right_ref, taps_ref, bias_ref, gain_ref, shift_ref,
    out_ref, slab, taps, total,
):
    rows, cols, chans = mid_ref.shape
    wide = 16
    block = 16
    taps[pl.ds(0, 49), :] = taps_ref[...].astype(F32)

    def chunk_step(chunk, carry):
        lanes = pl.ds(pl.multiple_of(chunk * LANES, LANES), LANES)
        for row in range(3):
            slab[pl.ds(row * wide + 3, cols), :] = low_ref[row, :, lanes].astype(F32)
            slab[pl.ds((rows + 3 + row) * wide + 3, cols), :] = high_ref[row, :, lanes].astype(F32)
        for row in range(rows):
            slab[pl.ds((row + 3) * wide + 3, cols), :] = mid_ref[row, :, lanes].astype(F32)
        for col in range(3):
            slab[pl.ds(col, rows + 6, stride=wide), :] = left_ref[col, :, lanes].astype(F32)
            slab[pl.ds(cols + 3 + col, rows + 6, stride=wide), :] = right_ref[col, :, lanes].astype(F32)
        for base in range(0, rows, block):
            start = jnp.broadcast_to(bias_ref[:, lanes], (cols, LANES))
            sums = [start] * block
            for b in range(7):
                weights = [jnp.broadcast_to(taps[pl.ds(7 * a + b, 1), lanes], (cols, LANES)) for a in range(7)]
                for row in range(block + 6):
                    window = slab[pl.ds((base + row) * wide + b, cols), :]
                    for a in range(7):
                        if 0 <= row - a < block:
                            sums[row - a] = sums[row - a] + window * weights[a]
            for row in range(block):
                total[pl.ds((base + row) * cols, cols), lanes] = sums[row]
        return carry

    lax.fori_loop(0, chans // LANES, chunk_step, 0)

    step = 64
    for base in range(0, rows * cols, step):
        part = pl.ds(base, step)
        values = total[part, :]
        centre = jnp.mean(values, axis=-1, keepdims=True)
        values = values - centre
        spread = jnp.mean(values * values, axis=-1, keepdims=True)
        total[part, :] = values * lax.rsqrt(spread + 1e-06)
    for place in range(chans // LANES):
        lanes = pl.ds(pl.multiple_of(order_ref[place] * LANES, LANES), LANES)
        out_ref[:, pl.ds(place * LANES, LANES)] = (
            total[:, lanes] * gain_ref[:, lanes] + shift_ref[:, lanes]
        ).astype(BF16)


def conv_norm(order, mid, low, high, left, right, taps, bias, gain, offset):
    rows, cols, chans = mid.shape
    return pl.pallas_call(
        conv_kernel,
        out_shape=jax.ShapeDtypeStruct((rows * cols, chans), BF16),
        in_specs=[SMEM] + [VMEM] * 9,
        out_specs=VMEM,
        scratch_shapes=[
            pltpu.VMEM(((rows + 6) * 16, LANES), F32),
            pltpu.VMEM((56, chans), F32),
            pltpu.VMEM((rows * cols, chans), F32),
        ],
        compiler_params=PARAMS,
        cost_estimate=pl.CostEstimate(flops=100 * rows * cols * chans, bytes_accessed=2 << 20, transcendentals=0),
    )(order, mid, low, high, left, right, taps, bias, gain, offset)


def up_kernel(parts, *refs):
    pixels, shards, bias_ref = refs[:parts], refs[parts:-parts - 2], refs[-parts - 2]
    outs, weight = refs[-parts - 1:-1], refs[-1]
    at = 0
    for shard in shards:
        weight[pl.ds(at, shard.shape[0]), :] = shard[...]
        at += shard.shape[0]
    hidden = weight.shape[1]
    for pixel, out in zip(pixels, outs):
        for n in range(0, hidden, 256):
            cols = pl.ds(n, 256)
            pre = jnp.dot(pixel[...], weight[:, cols], preferred_element_type=F32) + bias_ref[:, cols]
            out[:, cols] = (0.5 * pre * (1.0 + lax.erf(pre * 0.7071067811865476))).astype(BF16)


def up(pixels, shards, bias):
    depth = sum(s.shape[0] for s in shards)
    hidden = shards[0].shape[1]
    outs = tuple(jax.ShapeDtypeStruct((p.shape[0], hidden), BF16) for p in pixels)
    return pl.pallas_call(
        functools.partial(up_kernel, len(pixels)),
        out_shape=outs,
        in_specs=[VMEM] * (len(pixels) + len(shards) + 1),
        out_specs=tuple(VMEM for _ in outs),
        scratch_shapes=[pltpu.VMEM((depth, hidden), BF16)],
        compiler_params=PARAMS,
        cost_estimate=pl.CostEstimate(
            flops=2 * depth * hidden * sum(p.shape[0] for p in pixels), bytes_accessed=6 << 20, transcendentals=0
        ),
    )(*pixels, *shards, bias)


def down_kernel(parts, *refs):
    hidden, shards, outs = refs[:parts], refs[parts:-parts], refs[-parts:]
    for act, out in zip(hidden, outs):
        at = 0
        for shard in shards:
            count = shard.shape[0]
            out[:, pl.ds(at, count)] = lax.dot_general(
                act[...], shard[...], (((1,), (1,)), ((), ())), preferred_element_type=F32
            ).astype(BF16)
            at += count


def down(hidden, shards):
    chans = sum(s.shape[0] for s in shards)
    outs = tuple(jax.ShapeDtypeStruct((h.shape[0], chans), BF16) for h in hidden)
    return pl.pallas_call(
        functools.partial(down_kernel, len(hidden)),
        out_shape=outs,
        in_specs=[VMEM] * (len(hidden) + len(shards)),
        out_specs=tuple(VMEM for _ in outs),
        compiler_params=PARAMS,
        cost_estimate=pl.CostEstimate(
            flops=2 * chans * hidden[0].shape[1] * sum(h.shape[0] for h in hidden), bytes_accessed=6 << 20,
            transcendentals=0,
        ),
    )(*hidden, *shards)


def add_kernel(one_ref, two_ref, out_ref):
    out_ref[...] = (one_ref[...].astype(F32) + two_ref[...].astype(F32)).astype(BF16)


def add(one, two):
    return pl.pallas_call(
        add_kernel,
        out_shape=jax.ShapeDtypeStruct(one.shape, BF16),
        in_specs=[VMEM, VMEM],
        out_specs=VMEM,
        compiler_params=PARAMS,
    )(one, two)


def finish_kernel(order_ref, feature_ref, one_ref, two_ref, three_ref, bias_ref, scale_ref, out_ref):
    for place in range(feature_ref.shape[1] // LANES):
        lanes = pl.ds(pl.multiple_of(order_ref[place] * LANES, LANES), LANES)
        held = pl.ds(place * LANES, LANES)
        branch = (one_ref[:, held].astype(F32) + two_ref[:, held].astype(F32)) + three_ref[:, held].astype(F32)
        out_ref[:, lanes] = (
            feature_ref[:, lanes].astype(F32) + scale_ref[:, lanes] * (branch + bias_ref[:, lanes])
        ).astype(BF16)


def finish(order, features, one, two, three, bias, scale):
    return pl.pallas_call(
        finish_kernel,
        out_shape=jax.ShapeDtypeStruct(features.shape, BF16),
        in_specs=[SMEM] + [VMEM] * 6,
        out_specs=VMEM,
        compiler_params=PARAMS,
    )(order, features, one, two, three, bias, scale)


def spread(weight):
    count = lax.axis_size("lon")
    if weight.shape[0] != LANES:
        whole = lax.all_gather(weight, "lon", axis=0, tiled=True)
        return [whole]
    held = []
    for step in range(count // 2):
        mine = weight if step == 0 else shift(weight, "lon", step, 2)
        held += [mine, swap(mine, "lon", 1)]
    return held


def chunk_order(weight):
    count = lax.axis_size("lon")
    if weight.shape[0] != LANES:
        return jnp.arange(count * weight.shape[0] // LANES, dtype=jnp.int32)
    me = lax.axis_index("lon").astype(jnp.int32)
    group, side = me // 2, me % 2
    return jnp.stack(
        [((group - step) % (count // 2)) * 2 + (side ^ flip) for step in range(count // 2) for flip in range(2)]
    ).astype(jnp.int32)


def local(
    features,
    depth_kernel,
    depth_bias,
    norm_gain,
    norm_bias,
    up_weight,
    up_bias,
    down_weight,
    down_bias,
    layer_scale,
):
    rows, cols, chans = features.shape
    lats, lons = lax.axis_size("lat"), lax.axis_size("lon")
    line = lambda v: v.reshape(1, -1)

    forward = [(i, i + 1) for i in range(lats - 1)]
    low = lax.ppermute(features[rows - 3:], "lat", forward)
    high = lax.ppermute(features[:3], "lat", [(b, a) for a, b in forward])
    first, last = edges(low, features, high)
    left = lax.ppermute(last, "lon", [(i, (i + 1) % lons) for i in range(lons)])
    right = lax.ppermute(first, "lon", [((i + 1) % lons, i) for i in range(lons)])

    up_shards = spread(up_weight)
    down_shards = spread(down_weight)
    order = chunk_order(up_weight)

    normed = conv_norm(
        order, features, low, high, left, right, depth_kernel.reshape(49, chans),
        line(depth_bias), line(norm_gain), line(norm_bias),
    )
    across = swap(normed, "lat", 2)
    beside = swap(normed, "lat", 1)
    opposite = swap(across, "lat", 1)
    hid_opposite, hid_across, hid_beside, hid_own = up(
        [opposite, across, beside, normed], up_shards, line(up_bias)
    )
    far_opposite, far_across = down([hid_opposite, hid_across], down_shards)
    far = add(far_across, swap(far_opposite, "lat", 1))
    arrived = swap(far, "lat", 2)
    near_beside, near_own = down([hid_beside, hid_own], down_shards)
    near = swap(near_beside, "lat", 1)
    updated = finish(
        order, features.reshape(rows * cols, chans), near_own, near, arrived, line(down_bias), line(layer_scale)
    )
    return updated.reshape(rows, cols, chans)


def solution(mesh):
    placed = (
        P("lat", "lon", None),
        P(),
        P(),
        P(),
        P(),
        P("lon", "lat"),
        P("lat"),
        P("lon", "lat"),
        P(),
        P(),
    )
    return jax.shard_map(
        local, mesh=mesh, in_specs=placed, out_specs=P("lat", "lon", None), check_vma=False
    )
```

```python
import functools

import jax
import jax.numpy as jnp
from jax import lax
from jax.experimental import pallas as pl
from jax.experimental.pallas import tpu as pltpu
from jax.sharding import PartitionSpec as P

F32 = jnp.float32
BF16 = jnp.bfloat16
LANES = 128
VMEM = pl.BlockSpec(memory_space=pltpu.VMEM)
SMEM = pl.BlockSpec(memory_space=pltpu.SMEM)
PARAMS = pltpu.CompilerParams(vmem_limit_bytes=40 * 1024 * 1024)


def shift(value, axis, step, inner):
    count = lax.axis_size(axis)
    return lax.ppermute(value, axis, [(i, (i + step * inner) % count) for i in range(count)])


def swap(value, axis, bit):
    count = lax.axis_size(axis)
    return lax.ppermute(value, axis, [(i, i ^ bit) for i in range(count)])


def edges_kernel(mid_ref, first_ref, last_ref, slab):
    rows, cols, chans = mid_ref.shape
    for at in range(0, chans, LANES):
        lanes = pl.ds(at, LANES)
        slab[...] = mid_ref[:, :, lanes].astype(F32).reshape(rows * cols, LANES)
        for col in range(3):
            first_ref[col, :, lanes] = slab[pl.ds(col, rows, stride=cols), :].astype(BF16)
            last_ref[col, :, lanes] = slab[pl.ds(cols - 3 + col, rows, stride=cols), :].astype(BF16)


def edges(mid):
    rows, cols, chans = mid.shape
    block = 256
    shape = jax.ShapeDtypeStruct((3, rows, chans), BF16)
    out = pl.BlockSpec((3, rows, block), lambda i: (0, 0, i))
    return pl.pallas_call(
        edges_kernel,
        grid=(chans // block,),
        out_shape=(shape, shape),
        in_specs=[pl.BlockSpec((rows, cols, block), lambda i: (0, 0, i))],
        out_specs=(out, out),
        scratch_shapes=[pltpu.VMEM((rows * cols, LANES), F32)],
        compiler_params=PARAMS,
    )(mid)


WIDE = 16


def rims_kernel(mid_ref, left_ref, right_ref, top_ref, bottom_ref, slab):
    rows, cols, chans = mid_ref.shape
    slab[...] = jnp.zeros_like(slab)

    @pl.loop(0, chans // LANES)
    def _(chunk):
        lanes = pl.ds(pl.multiple_of(chunk * LANES, LANES), LANES)
        for out_ref, near, begin in ((top_ref, 0, 0), (bottom_ref, rows - 16, 13)):
            for row in range(3):
                slab[pl.ds(row * WIDE + 3, cols), :] = mid_ref[near + begin + row, :, lanes].astype(F32)
            for col in range(3):
                for at, ref in ((col, left_ref), (cols + 3 + col, right_ref)):
                    edge = ref[col, pl.ds(near, 16), lanes].astype(F32)
                    slab[pl.ds(at, 3, stride=WIDE), :] = edge[begin:begin + 3]
            out_ref[:, lanes] = slab[...].astype(BF16)


def rims(mid, left, right):
    chans = mid.shape[2]
    shape = jax.ShapeDtypeStruct((3 * WIDE, chans), BF16)
    return pl.pallas_call(
        rims_kernel,
        out_shape=(shape, shape),
        in_specs=[VMEM] * 3,
        out_specs=(VMEM, VMEM),
        scratch_shapes=[pltpu.VMEM((3 * WIDE, LANES), F32)],
        compiler_params=PARAMS,
    )(mid, left, right)


def conv_kernel(
    order_ref, mid_ref, low_ref, high_ref, left_ref, right_ref, taps_ref, bias_ref, gain_ref, shift_ref,
    out_ref, slab, taps, total,
):
    rows, cols, chans = mid_ref.shape
    block = 16
    taps[pl.ds(0, 49), :] = taps_ref[...].astype(F32)

    def chunk_step(chunk, carry):
        lanes = pl.ds(pl.multiple_of(chunk * LANES, LANES), LANES)
        slab[pl.ds(0, 3 * WIDE), :] = low_ref[:, lanes].astype(F32)
        slab[pl.ds((rows + 3) * WIDE, 3 * WIDE), :] = high_ref[:, lanes].astype(F32)
        for row in range(rows):
            slab[pl.ds((row + 3) * WIDE + 3, cols), :] = mid_ref[row, :, lanes].astype(F32)
        for col in range(3):
            slab[pl.ds(3 * WIDE + col, rows, stride=WIDE), :] = left_ref[col, :, lanes].astype(F32)
            slab[pl.ds(3 * WIDE + cols + 3 + col, rows, stride=WIDE), :] = right_ref[col, :, lanes].astype(F32)
        for base in range(0, rows, block):
            start = jnp.broadcast_to(bias_ref[:, lanes], (cols, LANES))
            sums = [start] * block
            for b in range(7):
                weights = [jnp.broadcast_to(taps[pl.ds(7 * a + b, 1), lanes], (cols, LANES)) for a in range(7)]
                for row in range(block + 6):
                    window = slab[pl.ds((base + row) * WIDE + b, cols), :]
                    for a in range(7):
                        if 0 <= row - a < block:
                            sums[row - a] = sums[row - a] + window * weights[a]
            for row in range(block):
                total[pl.ds((base + row) * cols, cols), lanes] = sums[row]
        return carry

    lax.fori_loop(0, chans // LANES, chunk_step, 0)

    step = 64
    for base in range(0, rows * cols, step):
        part = pl.ds(base, step)
        values = total[part, :]
        centre = jnp.mean(values, axis=-1, keepdims=True)
        values = values - centre
        spread = jnp.mean(values * values, axis=-1, keepdims=True)
        total[part, :] = values * lax.rsqrt(spread + 1e-06)
    for place in range(chans // LANES):
        lanes = pl.ds(pl.multiple_of(order_ref[place] * LANES, LANES), LANES)
        out_ref[:, pl.ds(place * LANES, LANES)] = (
            total[:, lanes] * gain_ref[:, lanes] + shift_ref[:, lanes]
        ).astype(BF16)


def conv_norm(order, mid, low, high, left, right, taps, bias, gain, offset):
    rows, cols, chans = mid.shape
    return pl.pallas_call(
        conv_kernel,
        out_shape=jax.ShapeDtypeStruct((rows * cols, chans), BF16),
        in_specs=[SMEM] + [VMEM] * 9,
        out_specs=VMEM,
        scratch_shapes=[
            pltpu.VMEM(((rows + 6) * WIDE, LANES), F32),
            pltpu.VMEM((56, chans), F32),
            pltpu.VMEM((rows * cols, chans), F32),
        ],
        compiler_params=PARAMS,
        cost_estimate=pl.CostEstimate(flops=100 * rows * cols * chans, bytes_accessed=2 << 20, transcendentals=0),
    )(order, mid, low, high, left, right, taps, bias, gain, offset)


def up_kernel(parts, spans, *refs):
    pixels, shards, bias_ref = refs[:parts], refs[parts:-parts - 2], refs[-parts - 2]
    outs, weight = refs[-parts - 1:-1], refs[-1]
    at = 0
    for shard, (start, count) in zip(shards, spans):
        weight[pl.ds(at, count), :] = shard[pl.ds(start, count), :]
        at += count
    hidden = weight.shape[1]
    for pixel, out in zip(pixels, outs):
        for n in range(0, hidden, 256):
            cols = pl.ds(n, 256)
            pre = jnp.dot(pixel[...], weight[:, cols], preferred_element_type=F32) + bias_ref[:, cols]
            out[:, cols] = (0.5 * pre * (1.0 + lax.erf(pre * 0.7071067811865476))).astype(BF16)


def up(pixels, shards, bias):
    arrays, spans = [s[0] for s in shards], tuple(s[1:] for s in shards)
    depth = sum(count for _, count in spans)
    hidden = arrays[0].shape[1]
    outs = tuple(jax.ShapeDtypeStruct((p.shape[0], hidden), BF16) for p in pixels)
    return pl.pallas_call(
        functools.partial(up_kernel, len(pixels), spans),
        out_shape=outs,
        in_specs=[VMEM] * (len(pixels) + len(shards) + 1),
        out_specs=tuple(VMEM for _ in outs),
        scratch_shapes=[pltpu.VMEM((depth, hidden), BF16)],
        compiler_params=PARAMS,
        cost_estimate=pl.CostEstimate(
            flops=2 * depth * hidden * sum(p.shape[0] for p in pixels), bytes_accessed=6 << 20, transcendentals=0
        ),
    )(*pixels, *arrays, bias)


def down_kernel(parts, spans, *refs):
    hidden, shards, outs = refs[:parts], refs[parts:-parts], refs[-parts:]
    for act, out in zip(hidden, outs):
        at = 0
        for shard, (start, count) in zip(shards, spans):
            out[:, pl.ds(at, count)] = lax.dot_general(
                act[...], shard[pl.ds(start, count), :], (((1,), (1,)), ((), ())), preferred_element_type=F32
            ).astype(BF16)
            at += count


def down(hidden, shards):
    arrays, spans = [s[0] for s in shards], tuple(s[1:] for s in shards)
    chans = sum(count for _, count in spans)
    outs = tuple(jax.ShapeDtypeStruct((h.shape[0], chans), BF16) for h in hidden)
    return pl.pallas_call(
        functools.partial(down_kernel, len(hidden), spans),
        out_shape=outs,
        in_specs=[VMEM] * (len(hidden) + len(shards)),
        out_specs=tuple(VMEM for _ in outs),
        compiler_params=PARAMS,
        cost_estimate=pl.CostEstimate(
            flops=2 * chans * hidden[0].shape[1] * sum(h.shape[0] for h in hidden), bytes_accessed=6 << 20,
            transcendentals=0,
        ),
    )(*hidden, *arrays)


def add_kernel(one_ref, two_ref, out_ref):
    out_ref[...] = (one_ref[...].astype(F32) + two_ref[...].astype(F32)).astype(BF16)


def add(one, two):
    return pl.pallas_call(
        add_kernel,
        out_shape=jax.ShapeDtypeStruct(one.shape, BF16),
        in_specs=[VMEM, VMEM],
        out_specs=VMEM,
        compiler_params=PARAMS,
    )(one, two)


def settle(feature, one, two, three, bias, scale):
    branch = (one.astype(F32) + two.astype(F32)) + three.astype(F32)
    return (feature.astype(F32) + scale * (branch + bias)).astype(BF16)


def part_kernel(first, order_ref, feature_ref, one_ref, two_ref, three_ref, bias_ref, scale_ref, out_ref):
    for at in range(0, out_ref.shape[1], LANES):
        lanes = pl.ds(pl.multiple_of(order_ref[first + at // LANES] * LANES, LANES), LANES)
        held = pl.ds(at, LANES)
        out_ref[:, held] = settle(
            feature_ref[:, lanes], one_ref[:, held], two_ref[:, held], three_ref[:, held],
            bias_ref[:, lanes], scale_ref[:, lanes],
        )


def part(first, order, features, group, bias, scale):
    return pl.pallas_call(
        functools.partial(part_kernel, first),
        out_shape=jax.ShapeDtypeStruct(group[0].shape, BF16),
        in_specs=[SMEM] + [VMEM] * 6,
        out_specs=VMEM,
        compiler_params=PARAMS,
    )(order, features, *group, bias, scale)


def finish_kernel(done, order_ref, feature_ref, *refs):
    parts, (one_ref, two_ref, three_ref, bias_ref, scale_ref, out_ref) = refs[:done], refs[done:]
    place = 0
    for part_ref in parts:
        for at in range(0, part_ref.shape[1], LANES):
            lanes = pl.ds(pl.multiple_of(order_ref[place] * LANES, LANES), LANES)
            out_ref[:, lanes] = part_ref[:, pl.ds(at, LANES)]
            place += 1
    for at in range(0, one_ref.shape[1], LANES):
        lanes = pl.ds(pl.multiple_of(order_ref[place] * LANES, LANES), LANES)
        held = pl.ds(at, LANES)
        out_ref[:, lanes] = settle(
            feature_ref[:, lanes], one_ref[:, held], two_ref[:, held], three_ref[:, held],
            bias_ref[:, lanes], scale_ref[:, lanes],
        )
        place += 1


def finish(order, features, sums, bias, scale):
    parts, place = [], 0
    for group in sums[:-1]:
        parts.append(part(place, order, features, group, bias, scale))
        place += group[0].shape[1] // LANES
    return pl.pallas_call(
        functools.partial(finish_kernel, len(parts)),
        out_shape=jax.ShapeDtypeStruct(features.shape, BF16),
        in_specs=[SMEM] + [VMEM] * (len(parts) + 6),
        out_specs=VMEM,
        compiler_params=PARAMS,
    )(order, features, *parts, *sums[-1], bias, scale)


def after(value, *earlier):
    return lax.optimization_barrier((value,) + earlier)[0]


STEPS = (0, 1, 3, 2)


def chunk_order(weight):
    count = lax.axis_size("lon")
    if weight.shape[0] != LANES:
        return jnp.arange(count * weight.shape[0] // LANES, dtype=jnp.int32)
    me = lax.axis_index("lon").astype(jnp.int32)
    group, side = me // 2, me % 2
    return jnp.stack(
        [((group - step) % (count // 2)) * 2 + (side ^ flip) for step in STEPS for flip in range(2)]
    ).astype(jnp.int32)


def local(
    features,
    depth_kernel,
    depth_bias,
    norm_gain,
    norm_bias,
    up_weight,
    up_bias,
    down_weight,
    down_bias,
    layer_scale,
):
    rows, cols, chans = features.shape
    lats, lons = lax.axis_size("lat"), lax.axis_size("lon")
    line = lambda v: v.reshape(1, -1)

    forward = [(i, i + 1) for i in range(lats - 1)]
    order = chunk_order(up_weight)
    conv_args = (depth_kernel.reshape(49, chans), line(depth_bias), line(norm_gain), line(norm_bias))
    z_of = lambda w, k: shift(w, "lon", k, 2)
    x_of = lambda w: swap(w, "lon", 1)
    if up_weight.shape[0] == LANES:
        both = jnp.concatenate([up_weight, down_weight], axis=0)
        first, last = edges(features)
        left = lax.ppermute(last, "lon", [(i, (i + 1) % lons) for i in range(lons)])
        right = lax.ppermute(first, "lon", [((i + 1) % lons, i) for i in range(lons)])
        top, bottom = rims(features, left, right)
        low = lax.ppermute(bottom, "lat", forward)
        high = lax.ppermute(top, "lat", [(b, a) for a, b in forward])
        uz1 = z_of(after(up_weight, first), 1)
        x0 = x_of(after(both, left))
        z3 = z_of(after(both, left), 3)
        uz2 = z_of(after(uz1, low), 1)
        ux1 = x_of(after(uz1, high))
        x3 = x_of(after(z3, ux1))
        ux2 = x_of(after(uz2, x0))
        dz1 = z_of(jnp.concatenate([after(down_weight, uz2), x0[LANES:]], axis=0), 1)
        dz2 = z_of(dz1, 1)
        normed = conv_norm(order, features, low, high, left, right, *conv_args)
        across = swap(normed, "lat", 2)
        beside = swap(after(normed, x0, ux1, uz2), "lat", 1)
        opposite = swap(after(across, beside, x3), "lat", 1)
        up_shards = [(up_weight, 0, LANES), (x0, 0, LANES), (uz1, 0, LANES), (ux1, 0, LANES), (z3, 0, LANES), (x3, 0, LANES), (uz2, 0, LANES), (ux2, 0, LANES)]
        hid_opposite, hid_across, hid_beside, hid_own = up([opposite, across, beside, normed], up_shards, line(up_bias))
        down_a = [(down_weight, 0, LANES), (x0, LANES, LANES), (dz1, 0, 2 * LANES), (z3, LANES, LANES), (x3, LANES, LANES)]
        far_opp_a, = down([hid_opposite], down_a)
        far_acr_a, = down([hid_across], down_a)
        far_in_a = swap(far_opp_a, "lat", 1)
        far_a = add(far_acr_a, far_in_a)
        arrived_a = swap(far_a, "lat", 2)
        near_bes_a, near_own_a = down([hid_beside, hid_own], down_a)
        near_in_a = swap(near_bes_a, "lat", 1)
        down_b = [(dz2, 0, 2 * LANES)]
        far_opp_b, = down([hid_opposite], down_b)
        far_acr_b, = down([hid_across], down_b)
        far_in_b = swap(far_opp_b, "lat", 1)
        far_b = add(far_acr_b, far_in_b)
        arrived_b = swap(far_b, "lat", 2)
        near_bes_b, near_own_b = down([hid_beside, hid_own], down_b)
        near_in_b = swap(near_bes_b, "lat", 1)
        sums = [(near_own_a, near_in_a, arrived_a), (near_own_b, near_in_b, arrived_b)]
    else:
        up_shards = [(lax.all_gather(up_weight, "lon", axis=0, tiled=True), 0, chans)]
        down_a = [(lax.all_gather(down_weight, "lon", axis=0, tiled=True), 0, chans)]
        first, last = edges(features)
        left = lax.ppermute(last, "lon", [(i, (i + 1) % lons) for i in range(lons)])
        right = lax.ppermute(first, "lon", [((i + 1) % lons, i) for i in range(lons)])
        top, bottom = rims(features, left, right)
        low = lax.ppermute(bottom, "lat", forward)
        high = lax.ppermute(top, "lat", [(b, a) for a, b in forward])
        normed = conv_norm(order, features, low, high, left, right, *conv_args)
        across = swap(normed, "lat", 2)
        beside = swap(normed, "lat", 1)
        opposite = swap(across, "lat", 1)
        hid_opposite, hid_across, hid_beside, hid_own = up([opposite, across, beside, normed], up_shards, line(up_bias))
        far_opp_a, = down([hid_opposite], down_a)
        far_acr_a, = down([hid_across], down_a)
        far_in_a = swap(far_opp_a, "lat", 1)
        far_a = add(far_acr_a, far_in_a)
        arrived_a = swap(far_a, "lat", 2)
        near_bes_a, near_own_a = down([hid_beside, hid_own], down_a)
        near_in_a = swap(near_bes_a, "lat", 1)
        sums = [(near_own_a, near_in_a, arrived_a)]
    updated = finish(
        order, features.reshape(rows * cols, chans), sums, line(down_bias), line(layer_scale)
    )
    return updated.reshape(rows, cols, chans)


def solution(mesh):
    placed = (
        P("lat", "lon", None),
        P(),
        P(),
        P(),
        P(),
        P("lon", "lat"),
        P("lat"),
        P("lon", "lat"),
        P(),
        P(),
    )
    return jax.shard_map(
        local, mesh=mesh, in_specs=placed, out_specs=P("lat", "lon", None), check_vma=False
    )
```

```python
import functools

import jax
import jax.numpy as jnp
from jax import lax
from jax.experimental import pallas as pl
from jax.experimental.pallas import tpu as pltpu
from jax.sharding import PartitionSpec as P

F32 = jnp.float32
BF16 = jnp.bfloat16
LANES = 128
VMEM = pl.BlockSpec(memory_space=pltpu.VMEM)
SMEM = pl.BlockSpec(memory_space=pltpu.SMEM)
PARAMS = pltpu.CompilerParams(vmem_limit_bytes=40 * 1024 * 1024)


def shift(value, axis, step, inner):
    count = lax.axis_size(axis)
    return lax.ppermute(value, axis, [(i, (i + step * inner) % count) for i in range(count)])


def swap(value, axis, bit):
    count = lax.axis_size(axis)
    return lax.ppermute(value, axis, [(i, i ^ bit) for i in range(count)])


def edges_kernel(mid_ref, first_ref, last_ref, slab):
    rows, cols, chans = mid_ref.shape
    for at in range(0, chans, LANES):
        lanes = pl.ds(at, LANES)
        slab[...] = mid_ref[:, :, lanes].astype(F32).reshape(rows * cols, LANES)
        for col in range(3):
            first_ref[col, :, lanes] = slab[pl.ds(col, rows, stride=cols), :].astype(BF16)
            last_ref[col, :, lanes] = slab[pl.ds(cols - 3 + col, rows, stride=cols), :].astype(BF16)


def edges(mid):
    rows, cols, chans = mid.shape
    block = 256
    shape = jax.ShapeDtypeStruct((3, rows, chans), BF16)
    out = pl.BlockSpec((3, rows, block), lambda i: (0, 0, i))
    return pl.pallas_call(
        edges_kernel,
        grid=(chans // block,),
        out_shape=(shape, shape),
        in_specs=[pl.BlockSpec((rows, cols, block), lambda i: (0, 0, i))],
        out_specs=(out, out),
        scratch_shapes=[pltpu.VMEM((rows * cols, LANES), F32)],
        compiler_params=PARAMS,
    )(mid)


WIDE = 16


def rims_kernel(mid_ref, left_ref, right_ref, top_ref, bottom_ref, slab):
    rows, cols, chans = mid_ref.shape
    slab[...] = jnp.zeros_like(slab)

    @pl.loop(0, chans // LANES)
    def _(chunk):
        lanes = pl.ds(pl.multiple_of(chunk * LANES, LANES), LANES)
        for out_ref, near, begin in ((top_ref, 0, 0), (bottom_ref, rows - 16, 13)):
            for row in range(3):
                slab[pl.ds(row * WIDE + 3, cols), :] = mid_ref[near + begin + row, :, lanes].astype(F32)
            for col in range(3):
                for at, ref in ((col, left_ref), (cols + 3 + col, right_ref)):
                    edge = ref[col, pl.ds(near, 16), lanes].astype(F32)
                    slab[pl.ds(at, 3, stride=WIDE), :] = edge[begin:begin + 3]
            out_ref[:, lanes] = slab[...].astype(BF16)


def rims(mid, left, right):
    chans = mid.shape[2]
    shape = jax.ShapeDtypeStruct((3 * WIDE, chans), BF16)
    return pl.pallas_call(
        rims_kernel,
        out_shape=(shape, shape),
        in_specs=[VMEM] * 3,
        out_specs=(VMEM, VMEM),
        scratch_shapes=[pltpu.VMEM((3 * WIDE, LANES), F32)],
        compiler_params=PARAMS,
    )(mid, left, right)


def conv_kernel(
    order_ref, mid_ref, low_ref, high_ref, left_ref, right_ref, taps_ref, bias_ref, gain_ref, shift_ref,
    out_ref, slab, taps, total,
):
    rows, cols, chans = mid_ref.shape
    block = 16
    taps[pl.ds(0, 49), :] = taps_ref[...].astype(F32)

    def chunk_step(chunk, carry):
        lanes = pl.ds(pl.multiple_of(chunk * LANES, LANES), LANES)
        slab[pl.ds(0, 3 * WIDE), :] = low_ref[:, lanes].astype(F32)
        slab[pl.ds((rows + 3) * WIDE, 3 * WIDE), :] = high_ref[:, lanes].astype(F32)
        for row in range(rows):
            slab[pl.ds((row + 3) * WIDE + 3, cols), :] = mid_ref[row, :, lanes].astype(F32)
        for col in range(3):
            slab[pl.ds(3 * WIDE + col, rows, stride=WIDE), :] = left_ref[col, :, lanes].astype(F32)
            slab[pl.ds(3 * WIDE + cols + 3 + col, rows, stride=WIDE), :] = right_ref[col, :, lanes].astype(F32)
        for base in range(0, rows, block):
            start = jnp.broadcast_to(bias_ref[:, lanes], (cols, LANES))
            sums = [start] * block
            for b in range(7):
                weights = [jnp.broadcast_to(taps[pl.ds(7 * a + b, 1), lanes], (cols, LANES)) for a in range(7)]
                for row in range(block + 6):
                    window = slab[pl.ds((base + row) * WIDE + b, cols), :]
                    for a in range(7):
                        if 0 <= row - a < block:
                            sums[row - a] = sums[row - a] + window * weights[a]
            for row in range(block):
                total[pl.ds((base + row) * cols, cols), lanes] = sums[row]
        return carry

    lax.fori_loop(0, chans // LANES, chunk_step, 0)

    step = 64
    for base in range(0, rows * cols, step):
        part = pl.ds(base, step)
        values = total[part, :]
        centre = jnp.mean(values, axis=-1, keepdims=True)
        values = values - centre
        spread = jnp.mean(values * values, axis=-1, keepdims=True)
        total[part, :] = values * lax.rsqrt(spread + 1e-06)
    for place in range(chans // LANES):
        lanes = pl.ds(pl.multiple_of(order_ref[place] * LANES, LANES), LANES)
        out_ref[:, pl.ds(place * LANES, LANES)] = (
            total[:, lanes] * gain_ref[:, lanes] + shift_ref[:, lanes]
        ).astype(BF16)


def conv_norm(order, mid, low, high, left, right, taps, bias, gain, offset):
    rows, cols, chans = mid.shape
    return pl.pallas_call(
        conv_kernel,
        out_shape=jax.ShapeDtypeStruct((rows * cols, chans), BF16),
        in_specs=[SMEM] + [VMEM] * 9,
        out_specs=VMEM,
        scratch_shapes=[
            pltpu.VMEM(((rows + 6) * WIDE, LANES), F32),
            pltpu.VMEM((56, chans), F32),
            pltpu.VMEM((rows * cols, chans), F32),
        ],
        compiler_params=PARAMS,
        cost_estimate=pl.CostEstimate(flops=100 * rows * cols * chans, bytes_accessed=2 << 20, transcendentals=0),
    )(order, mid, low, high, left, right, taps, bias, gain, offset)


def fill(weight, shards, spans):
    at = 0
    for shard, (start, count) in zip(shards, spans):
        weight[pl.ds(at, count), :] = shard[pl.ds(start, count), :]
        at += count


def begin_kernel(parts, spans, *refs):
    pixels, shards, bias_ref = refs[:parts], refs[parts:-parts - 2], refs[-parts - 2]
    outs, weight = refs[-parts - 1:-1], refs[-1]
    fill(weight, shards, spans)
    depth, hidden = weight.shape
    for pixel, out in zip(pixels, outs):
        for n in range(0, hidden, 256):
            cols = pl.ds(n, 256)
            out[:, cols] = (
                jnp.dot(pixel[:, pl.ds(0, depth)], weight[:, cols], preferred_element_type=F32) + bias_ref[:, cols]
            )


def begin(pixels, shards, bias):
    arrays, spans = [s[0] for s in shards], tuple(s[1:] for s in shards)
    depth = sum(count for _, count in spans)
    hidden = arrays[0].shape[1]
    outs = tuple(jax.ShapeDtypeStruct((p.shape[0], hidden), F32) for p in pixels)
    return pl.pallas_call(
        functools.partial(begin_kernel, len(pixels), spans),
        out_shape=outs,
        in_specs=[VMEM] * (len(pixels) + len(shards) + 1),
        out_specs=tuple(VMEM for _ in outs),
        scratch_shapes=[pltpu.VMEM((depth, hidden), BF16)],
        compiler_params=PARAMS,
        cost_estimate=pl.CostEstimate(
            flops=2 * depth * hidden * sum(p.shape[0] for p in pixels), bytes_accessed=1 << 20, transcendentals=0
        ),
    )(*pixels, *arrays, bias)


def up_kernel(parts, spans, *refs):
    pixels, sums, shards = refs[:parts], refs[parts:2 * parts], refs[2 * parts:-parts - 1]
    outs, weight = refs[-parts - 1:-1], refs[-1]
    fill(weight, shards, spans)
    depth, hidden = weight.shape
    for pixel, held, out in zip(pixels, sums, outs):
        rest = pl.ds(pixel.shape[1] - depth, depth)
        for n in range(0, hidden, 256):
            cols = pl.ds(n, 256)
            pre = held[:, cols] + jnp.dot(pixel[:, rest], weight[:, cols], preferred_element_type=F32)
            out[:, cols] = (0.5 * pre * (1.0 + lax.erf(pre * 0.7071067811865476))).astype(BF16)


def up(pixels, sums, shards):
    arrays, spans = [s[0] for s in shards], tuple(s[1:] for s in shards)
    depth = sum(count for _, count in spans)
    hidden = arrays[0].shape[1]
    outs = tuple(jax.ShapeDtypeStruct((p.shape[0], hidden), BF16) for p in pixels)
    return pl.pallas_call(
        functools.partial(up_kernel, len(pixels), spans),
        out_shape=outs,
        in_specs=[VMEM] * (2 * len(pixels) + len(shards)),
        out_specs=tuple(VMEM for _ in outs),
        scratch_shapes=[pltpu.VMEM((depth, hidden), BF16)],
        compiler_params=PARAMS,
        cost_estimate=pl.CostEstimate(
            flops=2 * depth * hidden * sum(p.shape[0] for p in pixels), bytes_accessed=1 << 20, transcendentals=0
        ),
    )(*pixels, *sums, *arrays)


def down_kernel(parts, spans, *refs):
    hidden, shards, outs = refs[:parts], refs[parts:-parts], refs[-parts:]
    for act, out in zip(hidden, outs):
        at = 0
        for shard, (start, count) in zip(shards, spans):
            out[:, pl.ds(at, count)] = lax.dot_general(
                act[...], shard[pl.ds(start, count), :], (((1,), (1,)), ((), ())), preferred_element_type=F32
            ).astype(BF16)
            at += count


def down(hidden, shards):
    arrays, spans = [s[0] for s in shards], tuple(s[1:] for s in shards)
    chans = sum(count for _, count in spans)
    outs = tuple(jax.ShapeDtypeStruct((h.shape[0], chans), BF16) for h in hidden)
    return pl.pallas_call(
        functools.partial(down_kernel, len(hidden), spans),
        out_shape=outs,
        in_specs=[VMEM] * (len(hidden) + len(shards)),
        out_specs=tuple(VMEM for _ in outs),
        compiler_params=PARAMS,
        cost_estimate=pl.CostEstimate(
            flops=2 * chans * hidden[0].shape[1] * sum(h.shape[0] for h in hidden), bytes_accessed=6 << 20,
            transcendentals=0,
        ),
    )(*hidden, *arrays)


def add_kernel(one_ref, two_ref, out_ref):
    out_ref[...] = (one_ref[...].astype(F32) + two_ref[...].astype(F32)).astype(BF16)


def add(one, two):
    return pl.pallas_call(
        add_kernel,
        out_shape=jax.ShapeDtypeStruct(one.shape, BF16),
        in_specs=[VMEM, VMEM],
        out_specs=VMEM,
        compiler_params=PARAMS,
    )(one, two)


def settle_kernel(first, order_ref, feature_ref, one_ref, two_ref, far_ref, bias_ref, scale_ref, *refs):
    out_ref, held, sems = refs[-3:]
    rows, chans = far_ref.shape
    copies = []
    for index in range(chans // LANES):
        lanes = pl.ds(pl.multiple_of(order_ref[first + index] * LANES, LANES), LANES)
        place = pl.ds(index * LANES, LANES)
        branch = (one_ref[:, place].astype(F32) + two_ref[:, place].astype(F32)) + far_ref[:, place].astype(F32)
        held[:, place] = (
            feature_ref[:, lanes].astype(F32) + scale_ref[:, lanes] * (branch + bias_ref[:, lanes])
        ).astype(BF16)
        copies.append(pltpu.make_async_copy(held.at[:, place], out_ref.at[:, lanes], sems.at[index]))
        copies[-1].start()
    for copy in copies:
        copy.wait()


def finish(order, features, groups, bias, scale):
    out, first = None, 0
    for one, two, far in groups:
        chans = far.shape[1]
        operands = (order, features, one, two, far, bias, scale)
        specs = [SMEM] + [VMEM] * 6
        if out is not None:
            operands, specs = operands + (out,), specs + [pl.BlockSpec(memory_space=pltpu.HBM)]
        out = pl.pallas_call(
            functools.partial(settle_kernel, first),
            out_shape=jax.ShapeDtypeStruct(features.shape, BF16),
            in_specs=specs,
            out_specs=pl.BlockSpec(memory_space=pltpu.HBM),
            scratch_shapes=[pltpu.VMEM(far.shape, BF16), pltpu.SemaphoreType.DMA((chans // LANES,))],
            input_output_aliases={7: 0} if out is not None else {},
            compiler_params=PARAMS,
        )(*operands)
        first += chans // LANES
    return out


def after(value, *earlier):
    return lax.optimization_barrier((value,) + earlier)[0]


STEPS = (0, 1, 3, 2)


def chunk_order(weight):
    count = lax.axis_size("lon")
    if weight.shape[0] != LANES:
        return jnp.arange(count * weight.shape[0] // LANES, dtype=jnp.int32)
    me = lax.axis_index("lon").astype(jnp.int32)
    group, side = me // 2, me % 2
    return jnp.stack(
        [((group - step) % (count // 2)) * 2 + (side ^ flip) for step in STEPS for flip in range(2)]
    ).astype(jnp.int32)


def local(
    features,
    depth_kernel,
    depth_bias,
    norm_gain,
    norm_bias,
    up_weight,
    up_bias,
    down_weight,
    down_bias,
    layer_scale,
):
    rows, cols, chans = features.shape
    lats, lons = lax.axis_size("lat"), lax.axis_size("lon")
    line = lambda v: v.reshape(1, -1)

    forward = [(i, i + 1) for i in range(lats - 1)]
    order = chunk_order(up_weight)
    conv_args = (depth_kernel.reshape(49, chans), line(depth_bias), line(norm_gain), line(norm_bias))
    z_of = lambda w, k: shift(w, "lon", k, 2)
    x_of = lambda w: swap(w, "lon", 1)
    if up_weight.shape[0] == LANES:
        both = jnp.concatenate([up_weight, down_weight], axis=0)
        first, last = edges(features)
        left = lax.ppermute(last, "lon", [(i, (i + 1) % lons) for i in range(lons)])
        right = lax.ppermute(first, "lon", [((i + 1) % lons, i) for i in range(lons)])
        top, bottom = rims(features, left, right)
        low = lax.ppermute(bottom, "lat", forward)
        high = lax.ppermute(top, "lat", [(b, a) for a, b in forward])
        uz1 = z_of(after(up_weight, first), 1)
        x0 = x_of(after(both, left))
        z3 = z_of(after(both, first), 3)
        uz2 = z_of(after(uz1, low), 1)
        ux1 = x_of(after(uz1, high))
        x3 = x_of(after(z3, ux1))
        ux2 = x_of(after(uz2, x0))
        dz1 = z_of(jnp.concatenate([after(down_weight, uz2), x0[LANES:]], axis=0), 1)
        dz2 = z_of(dz1, 1)
        normed = conv_norm(order, features, low, high, left, right, *conv_args)
        across = swap(normed, "lat", 2)
        beside = swap(after(normed, x0, ux1, uz2), "lat", 1)
        opposite = swap(after(across, beside, x3), "lat", 1)
        up_shards = [(up_weight, 0, LANES), (x0, 0, LANES), (uz1, 0, LANES), (ux1, 0, LANES), (z3, 0, LANES), (x3, 0, LANES), (uz2, 0, LANES), (ux2, 0, LANES)]
        sums = begin([after(opposite, dz1), across, beside, normed], up_shards[:-1], line(up_bias))
        hid_opposite, hid_across, hid_beside, hid_own = up([opposite, across, beside, normed], sums, up_shards[-1:])
        down_a = [(down_weight, 0, LANES), (x0, LANES, LANES), (dz1, 0, 2 * LANES), (z3, LANES, LANES), (x3, LANES, LANES)]
        far_opp_a, = down([hid_opposite], down_a)
        far_acr_a, = down([hid_across], down_a)
        far_in_a = swap(far_opp_a, "lat", 1)
        far_a = add(far_acr_a, far_in_a)
        arrived_a = swap(far_a, "lat", 2)
        near_bes_a, near_own_a = down([hid_beside, hid_own], down_a)
        near_in_a = swap(near_bes_a, "lat", 1)
        down_b = [(dz2, 0, 2 * LANES)]
        far_opp_b, = down([hid_opposite], down_b)
        far_acr_b, = down([hid_across], down_b)
        far_in_b = swap(far_opp_b, "lat", 1)
        far_b = add(far_acr_b, far_in_b)
        arrived_b = swap(far_b, "lat", 2)
        near_bes_b, near_own_b = down([hid_beside, hid_own], down_b)
        near_in_b = swap(near_bes_b, "lat", 1)
        groups = [(near_own_a, near_in_a, arrived_a), (near_own_b, near_in_b, arrived_b)]
    else:
        up_whole = lax.all_gather(up_weight, "lon", axis=0, tiled=True)
        up_shards = [(up_whole, 0, chans - LANES), (up_whole, chans - LANES, LANES)]
        down_a = [(lax.all_gather(down_weight, "lon", axis=0, tiled=True), 0, chans)]
        first, last = edges(features)
        left = lax.ppermute(last, "lon", [(i, (i + 1) % lons) for i in range(lons)])
        right = lax.ppermute(first, "lon", [((i + 1) % lons, i) for i in range(lons)])
        top, bottom = rims(features, left, right)
        low = lax.ppermute(bottom, "lat", forward)
        high = lax.ppermute(top, "lat", [(b, a) for a, b in forward])
        normed = conv_norm(order, features, low, high, left, right, *conv_args)
        across = swap(normed, "lat", 2)
        beside = swap(normed, "lat", 1)
        opposite = swap(across, "lat", 1)
        sums = begin([opposite, across, beside, normed], up_shards[:-1], line(up_bias))
        hid_opposite, hid_across, hid_beside, hid_own = up([opposite, across, beside, normed], sums, up_shards[-1:])
        far_opp_a, = down([hid_opposite], down_a)
        far_acr_a, = down([hid_across], down_a)
        far_in_a = swap(far_opp_a, "lat", 1)
        far_a = add(far_acr_a, far_in_a)
        arrived_a = swap(far_a, "lat", 2)
        near_bes_a, near_own_a = down([hid_beside, hid_own], down_a)
        near_in_a = swap(near_bes_a, "lat", 1)
        groups = [(near_own_a, near_in_a, arrived_a)]
    updated = finish(order, features.reshape(rows * cols, chans), groups, line(down_bias), line(layer_scale))
    return updated.reshape(rows, cols, chans)


def solution(mesh):
    placed = (
        P("lat", "lon", None),
        P(),
        P(),
        P(),
        P(),
        P("lon", "lat"),
        P("lat"),
        P("lon", "lat"),
        P(),
        P(),
    )
    return jax.shard_map(
        local, mesh=mesh, in_specs=placed, out_specs=P("lat", "lon", None), check_vma=False
    )
```

```python
import functools

import jax
import jax.numpy as jnp
from jax import lax
from jax.experimental import pallas as pl
from jax.experimental.pallas import tpu as pltpu
from jax.sharding import PartitionSpec as P

F32 = jnp.float32
BF16 = jnp.bfloat16
LANES = 128
VMEM = pl.BlockSpec(memory_space=pltpu.VMEM)
SMEM = pl.BlockSpec(memory_space=pltpu.SMEM)
PARAMS = pltpu.CompilerParams(vmem_limit_bytes=40 * 1024 * 1024)


def shift(value, axis, step, inner):
    count = lax.axis_size(axis)
    return lax.ppermute(value, axis, [(i, (i + step * inner) % count) for i in range(count)])


def swap(value, axis, bit):
    count = lax.axis_size(axis)
    return lax.ppermute(value, axis, [(i, i ^ bit) for i in range(count)])


def edges_kernel(mid_ref, first_ref, last_ref, slab):
    rows, cols, chans = mid_ref.shape
    for at in range(0, chans, LANES):
        lanes = pl.ds(at, LANES)
        slab[...] = mid_ref[:, :, lanes].astype(F32).reshape(rows * cols, LANES)
        for col in range(3):
            first_ref[col, :, lanes] = slab[pl.ds(col, rows, stride=cols), :].astype(BF16)
            last_ref[col, :, lanes] = slab[pl.ds(cols - 3 + col, rows, stride=cols), :].astype(BF16)


def edges(mid):
    rows, cols, chans = mid.shape
    block = 256
    shape = jax.ShapeDtypeStruct((3, rows, chans), BF16)
    out = pl.BlockSpec((3, rows, block), lambda i: (0, 0, i))
    return pl.pallas_call(
        edges_kernel,
        grid=(chans // block,),
        out_shape=(shape, shape),
        in_specs=[pl.BlockSpec((rows, cols, block), lambda i: (0, 0, i))],
        out_specs=(out, out),
        scratch_shapes=[pltpu.VMEM((rows * cols, LANES), F32)],
        compiler_params=PARAMS,
    )(mid)


WIDE = 16


def rims_kernel(mid_ref, left_ref, right_ref, top_ref, bottom_ref, slab):
    rows, cols, chans = mid_ref.shape
    slab[...] = jnp.zeros_like(slab)

    @pl.loop(0, chans // LANES)
    def _(chunk):
        lanes = pl.ds(pl.multiple_of(chunk * LANES, LANES), LANES)
        for out_ref, near, begin in ((top_ref, 0, 0), (bottom_ref, rows - 16, 13)):
            for row in range(3):
                slab[pl.ds(row * WIDE + 3, cols), :] = mid_ref[near + begin + row, :, lanes].astype(F32)
            for col in range(3):
                for at, ref in ((col, left_ref), (cols + 3 + col, right_ref)):
                    edge = ref[col, pl.ds(near, 16), lanes].astype(F32)
                    slab[pl.ds(at, 3, stride=WIDE), :] = edge[begin:begin + 3]
            out_ref[:, lanes] = slab[...].astype(BF16)


def rims(mid, left, right):
    chans = mid.shape[2]
    shape = jax.ShapeDtypeStruct((3 * WIDE, chans), BF16)
    return pl.pallas_call(
        rims_kernel,
        out_shape=(shape, shape),
        in_specs=[VMEM] * 3,
        out_specs=(VMEM, VMEM),
        scratch_shapes=[pltpu.VMEM((3 * WIDE, LANES), F32)],
        compiler_params=PARAMS,
    )(mid, left, right)


def conv_kernel(
    order_ref, mid_ref, low_ref, high_ref, left_ref, right_ref, taps_ref, bias_ref, gain_ref, shift_ref,
    out_ref, slab, taps, total,
):
    rows, cols, chans = mid_ref.shape
    block = 16
    taps[pl.ds(0, 49), :] = taps_ref[...].astype(F32)

    def chunk_step(chunk, carry):
        lanes = pl.ds(pl.multiple_of(chunk * LANES, LANES), LANES)
        slab[pl.ds(0, 3 * WIDE), :] = low_ref[:, lanes].astype(F32)
        slab[pl.ds((rows + 3) * WIDE, 3 * WIDE), :] = high_ref[:, lanes].astype(F32)
        for row in range(rows):
            slab[pl.ds((row + 3) * WIDE + 3, cols), :] = mid_ref[row, :, lanes].astype(F32)
        for col in range(3):
            slab[pl.ds(3 * WIDE + col, rows, stride=WIDE), :] = left_ref[col, :, lanes].astype(F32)
            slab[pl.ds(3 * WIDE + cols + 3 + col, rows, stride=WIDE), :] = right_ref[col, :, lanes].astype(F32)
        for base in range(0, rows, block):
            start = jnp.broadcast_to(bias_ref[:, lanes], (cols, LANES))
            sums = [start] * block
            for b in range(7):
                weights = [jnp.broadcast_to(taps[pl.ds(7 * a + b, 1), lanes], (cols, LANES)) for a in range(7)]
                for row in range(block + 6):
                    window = slab[pl.ds((base + row) * WIDE + b, cols), :]
                    for a in range(7):
                        if 0 <= row - a < block:
                            sums[row - a] = sums[row - a] + window * weights[a]
            for row in range(block):
                total[pl.ds((base + row) * cols, cols), lanes] = sums[row]
        return carry

    lax.fori_loop(0, chans // LANES, chunk_step, 0)

    step = 64
    for base in range(0, rows * cols, step):
        part = pl.ds(base, step)
        values = total[part, :]
        centre = jnp.mean(values, axis=-1, keepdims=True)
        values = values - centre
        spread = jnp.mean(values * values, axis=-1, keepdims=True)
        total[part, :] = values * lax.rsqrt(spread + 1e-06)
    for place in range(chans // LANES):
        lanes = pl.ds(pl.multiple_of(order_ref[place] * LANES, LANES), LANES)
        out_ref[:, pl.ds(place * LANES, LANES)] = (
            total[:, lanes] * gain_ref[:, lanes] + shift_ref[:, lanes]
        ).astype(BF16)


def conv_norm(order, mid, low, high, left, right, taps, bias, gain, offset):
    rows, cols, chans = mid.shape
    return pl.pallas_call(
        conv_kernel,
        out_shape=jax.ShapeDtypeStruct((rows * cols, chans), BF16),
        in_specs=[SMEM] + [VMEM] * 9,
        out_specs=VMEM,
        scratch_shapes=[
            pltpu.VMEM(((rows + 6) * WIDE, LANES), F32),
            pltpu.VMEM((56, chans), F32),
            pltpu.VMEM((rows * cols, chans), F32),
        ],
        compiler_params=PARAMS,
        cost_estimate=pl.CostEstimate(flops=100 * rows * cols * chans, bytes_accessed=2 << 20, transcendentals=0),
    )(order, mid, low, high, left, right, taps, bias, gain, offset)


def fill(weight, shards, spans):
    at = 0
    for shard, (start, count) in zip(shards, spans):
        weight[pl.ds(at, count), :] = shard[pl.ds(start, count), :]
        at += count


def begin_kernel(parts, spans, *refs):
    pixels, shards, bias_ref = refs[:parts], refs[parts:-parts - 2], refs[-parts - 2]
    outs, weight = refs[-parts - 1:-1], refs[-1]
    fill(weight, shards, spans)
    depth, hidden = weight.shape
    for pixel, out in zip(pixels, outs):
        for n in range(0, hidden, 256):
            cols = pl.ds(n, 256)
            out[:, cols] = (
                jnp.dot(pixel[:, pl.ds(0, depth)], weight[:, cols], preferred_element_type=F32) + bias_ref[:, cols]
            )


def begin(pixels, shards, bias):
    arrays, spans = [s[0] for s in shards], tuple(s[1:] for s in shards)
    depth = sum(count for _, count in spans)
    hidden = arrays[0].shape[1]
    outs = tuple(jax.ShapeDtypeStruct((p.shape[0], hidden), F32) for p in pixels)
    return pl.pallas_call(
        functools.partial(begin_kernel, len(pixels), spans),
        out_shape=outs,
        in_specs=[VMEM] * (len(pixels) + len(shards) + 1),
        out_specs=tuple(VMEM for _ in outs),
        scratch_shapes=[pltpu.VMEM((depth, hidden), BF16)],
        compiler_params=PARAMS,
        cost_estimate=pl.CostEstimate(
            flops=2 * depth * hidden * sum(p.shape[0] for p in pixels), bytes_accessed=1 << 20, transcendentals=0
        ),
    )(*pixels, *arrays, bias)


def up_kernel(parts, spans, *refs):
    pixels, sums, shards = refs[:parts], refs[parts:2 * parts], refs[2 * parts:-parts - 1]
    outs, weight = refs[-parts - 1:-1], refs[-1]
    fill(weight, shards, spans)
    depth, hidden = weight.shape
    for pixel, held, out in zip(pixels, sums, outs):
        rest = pl.ds(pixel.shape[1] - depth, depth)
        for n in range(0, hidden, 256):
            cols = pl.ds(n, 256)
            pre = held[:, cols] + jnp.dot(pixel[:, rest], weight[:, cols], preferred_element_type=F32)
            out[:, cols] = (0.5 * pre * (1.0 + lax.erf(pre * 0.7071067811865476))).astype(BF16)


def up(pixels, sums, shards):
    arrays, spans = [s[0] for s in shards], tuple(s[1:] for s in shards)
    depth = sum(count for _, count in spans)
    hidden = arrays[0].shape[1]
    outs = tuple(jax.ShapeDtypeStruct((p.shape[0], hidden), BF16) for p in pixels)
    return pl.pallas_call(
        functools.partial(up_kernel, len(pixels), spans),
        out_shape=outs,
        in_specs=[VMEM] * (2 * len(pixels) + len(shards)),
        out_specs=tuple(VMEM for _ in outs),
        scratch_shapes=[pltpu.VMEM((depth, hidden), BF16)],
        compiler_params=PARAMS,
        cost_estimate=pl.CostEstimate(
            flops=2 * depth * hidden * sum(p.shape[0] for p in pixels), bytes_accessed=1 << 20, transcendentals=0
        ),
    )(*pixels, *sums, *arrays)


def down_kernel(parts, spans, *refs):
    hidden, shards, outs = refs[:parts], refs[parts:-parts], refs[-parts:]
    for act, out in zip(hidden, outs):
        at = 0
        for shard, (start, count) in zip(shards, spans):
            out[:, pl.ds(at, count)] = lax.dot_general(
                act[...], shard[pl.ds(start, count), :], (((1,), (1,)), ((), ())), preferred_element_type=F32
            ).astype(BF16)
            at += count


def down(hidden, shards):
    arrays, spans = [s[0] for s in shards], tuple(s[1:] for s in shards)
    chans = sum(count for _, count in spans)
    outs = tuple(jax.ShapeDtypeStruct((h.shape[0], chans), BF16) for h in hidden)
    return pl.pallas_call(
        functools.partial(down_kernel, len(hidden), spans),
        out_shape=outs,
        in_specs=[VMEM] * (len(hidden) + len(shards)),
        out_specs=tuple(VMEM for _ in outs),
        compiler_params=PARAMS,
        cost_estimate=pl.CostEstimate(
            flops=2 * chans * hidden[0].shape[1] * sum(h.shape[0] for h in hidden), bytes_accessed=6 << 20,
            transcendentals=0,
        ),
    )(*hidden, *arrays)


def add_kernel(one_ref, two_ref, out_ref):
    out_ref[...] = (one_ref[...].astype(F32) + two_ref[...].astype(F32)).astype(BF16)


def add(one, two):
    return pl.pallas_call(
        add_kernel,
        out_shape=jax.ShapeDtypeStruct(one.shape, BF16),
        in_specs=[VMEM, VMEM],
        out_specs=VMEM,
        compiler_params=PARAMS,
    )(one, two)


def settle_kernel(first, order_ref, feature_ref, one_ref, two_ref, far_ref, bias_ref, scale_ref, *refs):
    out_ref, held, sems = refs[-3:]
    rows, chans = far_ref.shape
    copies = []
    for index in range(chans // LANES):
        lanes = pl.ds(pl.multiple_of(order_ref[first + index] * LANES, LANES), LANES)
        place = pl.ds(index * LANES, LANES)
        branch = (one_ref[:, place].astype(F32) + two_ref[:, place].astype(F32)) + far_ref[:, place].astype(F32)
        held[:, place] = (
            feature_ref[:, lanes].astype(F32) + scale_ref[:, lanes] * (branch + bias_ref[:, lanes])
        ).astype(BF16)
        copies.append(pltpu.make_async_copy(held.at[:, place], out_ref.at[:, lanes], sems.at[index]))
        copies[-1].start()
    for copy in copies:
        copy.wait()


def finish(order, features, groups, bias, scale):
    out, first = None, 0
    for one, two, far in groups:
        chans = far.shape[1]
        operands = (order, features, one, two, far, bias, scale)
        specs = [SMEM] + [VMEM] * 6
        if out is not None:
            operands, specs = operands + (out,), specs + [pl.BlockSpec(memory_space=pltpu.HBM)]
        out = pl.pallas_call(
            functools.partial(settle_kernel, first),
            out_shape=jax.ShapeDtypeStruct(features.shape, BF16),
            in_specs=specs,
            out_specs=pl.BlockSpec(memory_space=pltpu.HBM),
            scratch_shapes=[pltpu.VMEM(far.shape, BF16), pltpu.SemaphoreType.DMA((chans // LANES,))],
            input_output_aliases={7: 0} if out is not None else {},
            compiler_params=PARAMS,
        )(*operands)
        first += chans // LANES
    return out


def after(value, *earlier):
    return lax.optimization_barrier((value,) + earlier)[0]


STEPS = (0, 1, 3, 2)


def chunk_order(weight):
    count = lax.axis_size("lon")
    if weight.shape[0] != LANES:
        return jnp.arange(count * weight.shape[0] // LANES, dtype=jnp.int32)
    me = lax.axis_index("lon").astype(jnp.int32)
    group, side = me // 2, me % 2
    return jnp.stack(
        [((group - step) % (count // 2)) * 2 + (side ^ flip) for step in STEPS for flip in range(2)]
    ).astype(jnp.int32)


def local(
    features,
    depth_kernel,
    depth_bias,
    norm_gain,
    norm_bias,
    up_weight,
    up_bias,
    down_weight,
    down_bias,
    layer_scale,
):
    rows, cols, chans = features.shape
    lats, lons = lax.axis_size("lat"), lax.axis_size("lon")
    line = lambda v: v.reshape(1, -1)

    forward = [(i, i + 1) for i in range(lats - 1)]
    order = chunk_order(up_weight)
    conv_args = (depth_kernel.reshape(49, chans), line(depth_bias), line(norm_gain), line(norm_bias))
    z_of = lambda w, k: shift(w, "lon", k, 2)
    x_of = lambda w: swap(w, "lon", 1)
    if up_weight.shape[0] == LANES:
        both = jnp.concatenate([up_weight, down_weight], axis=0)
        first, last = edges(features)
        left = lax.ppermute(last, "lon", [(i, (i + 1) % lons) for i in range(lons)])
        right = lax.ppermute(first, "lon", [((i + 1) % lons, i) for i in range(lons)])
        top, bottom = rims(features, left, right)
        low = lax.ppermute(bottom, "lat", forward)
        high = lax.ppermute(top, "lat", [(b, a) for a, b in forward])
        uz1 = z_of(up_weight, 1)
        x0 = x_of(after(both, left))
        z3 = z_of(after(both, first), 3)
        uz2 = z_of(after(uz1, low), 1)
        ux1 = x_of(after(uz1, high))
        ux2 = x_of(after(uz2, x0))
        dz1 = z_of(jnp.concatenate([after(down_weight, uz2), x0[LANES:]], axis=0), 1)
        dz2 = z_of(dz1, 1)
        normed = conv_norm(order, features, after(low, top), high, left, right, *conv_args)
        x3 = x_of(after(z3, normed))
        across = swap(normed, "lat", 2)
        beside = swap(after(normed, ux1, uz2, x0), "lat", 1)
        opposite = swap(after(across, beside, x3), "lat", 1)
        up_shards = [(up_weight, 0, LANES), (x0, 0, LANES), (uz1, 0, LANES), (ux1, 0, LANES), (z3, 0, LANES), (x3, 0, LANES), (uz2, 0, LANES), (ux2, 0, LANES)]
        sums = begin([after(opposite, dz1), across, beside, normed], up_shards[:-1], line(up_bias))
        hid_opposite, hid_across, hid_beside, hid_own = up([opposite, across, beside, normed], sums, up_shards[-1:])
        down_a = [(down_weight, 0, LANES), (x0, LANES, LANES), (dz1, 0, 2 * LANES), (z3, LANES, LANES), (x3, LANES, LANES)]
        far_opp_a, = down([hid_opposite], down_a)
        far_acr_a, = down([hid_across], down_a)
        far_in_a = swap(far_opp_a, "lat", 1)
        far_a = add(far_acr_a, far_in_a)
        arrived_a = swap(far_a, "lat", 2)
        near_bes_a, = down([hid_beside], down_a)
        near_in_a = swap(near_bes_a, "lat", 1)
        near_own_a, = down([hid_own], down_a)
        down_b = [(dz2, 0, 2 * LANES)]
        far_opp_b, = down([hid_opposite], down_b)
        far_acr_b, = down([hid_across], down_b)
        far_in_b = swap(far_opp_b, "lat", 1)
        far_b = add(after(far_acr_b, far_a), far_in_b)
        arrived_b = swap(after(far_b, far_opp_a), "lat", 2)
        near_bes_b, = down([hid_beside], down_b)
        near_in_b = swap(near_bes_b, "lat", 1)
        near_own_b, = down([hid_own], down_b)
        groups = [(near_own_a, near_in_a, arrived_a), (near_own_b, near_in_b, arrived_b)]
    else:
        up_whole = lax.all_gather(up_weight, "lon", axis=0, tiled=True)
        up_shards = [(up_whole, 0, chans - LANES), (up_whole, chans - LANES, LANES)]
        down_a = [(lax.all_gather(down_weight, "lon", axis=0, tiled=True), 0, chans)]
        first, last = edges(features)
        left = lax.ppermute(last, "lon", [(i, (i + 1) % lons) for i in range(lons)])
        right = lax.ppermute(first, "lon", [((i + 1) % lons, i) for i in range(lons)])
        top, bottom = rims(features, left, right)
        low = lax.ppermute(bottom, "lat", forward)
        high = lax.ppermute(top, "lat", [(b, a) for a, b in forward])
        normed = conv_norm(order, features, low, high, left, right, *conv_args)
        across = swap(normed, "lat", 2)
        beside = swap(normed, "lat", 1)
        opposite = swap(across, "lat", 1)
        sums = begin([opposite, across, beside, normed], up_shards[:-1], line(up_bias))
        hid_opposite, hid_across, hid_beside, hid_own = up([opposite, across, beside, normed], sums, up_shards[-1:])
        far_opp_a, = down([hid_opposite], down_a)
        far_acr_a, = down([hid_across], down_a)
        far_in_a = swap(far_opp_a, "lat", 1)
        far_a = add(far_acr_a, far_in_a)
        arrived_a = swap(far_a, "lat", 2)
        near_bes_a, = down([hid_beside], down_a)
        near_in_a = swap(near_bes_a, "lat", 1)
        near_own_a, = down([hid_own], down_a)
        groups = [(near_own_a, near_in_a, arrived_a)]
    updated = finish(order, features.reshape(rows * cols, chans), groups, line(down_bias), line(layer_scale))
    return updated.reshape(rows, cols, chans)


def solution(mesh):
    placed = (
        P("lat", "lon", None),
        P(),
        P(),
        P(),
        P(),
        P("lon", "lat"),
        P("lat"),
        P("lon", "lat"),
        P(),
        P(),
    )
    return jax.shard_map(
        local, mesh=mesh, in_specs=placed, out_specs=P("lat", "lon", None), check_vma=False
    )
```

```python
import functools

import jax
import jax.numpy as jnp
from jax import lax
from jax.experimental import pallas as pl
from jax.experimental.pallas import tpu as pltpu
from jax.sharding import PartitionSpec as P

F32 = jnp.float32
BF16 = jnp.bfloat16
LANES = 128
VMEM = pl.BlockSpec(memory_space=pltpu.VMEM)
SMEM = pl.BlockSpec(memory_space=pltpu.SMEM)
PARAMS = pltpu.CompilerParams(vmem_limit_bytes=40 * 1024 * 1024)


def shift(value, axis, step, inner):
    count = lax.axis_size(axis)
    return lax.ppermute(value, axis, [(i, (i + step * inner) % count) for i in range(count)])


def swap(value, axis, bit):
    count = lax.axis_size(axis)
    return lax.ppermute(value, axis, [(i, i ^ bit) for i in range(count)])


def edges_kernel(mid_ref, first_ref, last_ref, slab):
    rows, cols, chans = mid_ref.shape
    for at in range(0, chans, LANES):
        lanes = pl.ds(at, LANES)
        slab[pl.ds(0, rows * cols), :] = mid_ref[:, :, lanes].astype(F32).reshape(rows * cols, LANES)
        for col in range(3):
            first_ref[col, :, lanes] = slab[pl.ds(col, rows, stride=cols), :].astype(BF16)
            last_ref[col, :, lanes] = slab[pl.ds(cols - 3 + col, rows, stride=cols), :].astype(BF16)


def edges(mid):
    rows, cols, chans = mid.shape
    block = 256
    shape = jax.ShapeDtypeStruct((3, rows, chans), BF16)
    out = pl.BlockSpec((3, rows, block), lambda i: (0, 0, i))
    return pl.pallas_call(
        edges_kernel,
        grid=(chans // block,),
        out_shape=(shape, shape),
        in_specs=[pl.BlockSpec((rows, cols, block), lambda i: (0, 0, i))],
        out_specs=(out, out),
        scratch_shapes=[pltpu.VMEM(((rows + 1) * cols, LANES), F32)],
        compiler_params=PARAMS,
    )(mid)


WIDE = 16


def rims_kernel(mid_ref, left_ref, right_ref, top_ref, bottom_ref, slab):
    rows, cols, chans = mid_ref.shape
    slab[...] = jnp.zeros_like(slab)

    @pl.loop(0, chans // LANES)
    def _(chunk):
        lanes = pl.ds(pl.multiple_of(chunk * LANES, LANES), LANES)
        for out_ref, near, begin in ((top_ref, 0, 0), (bottom_ref, rows - 16, 13)):
            for row in range(3):
                slab[pl.ds(row * WIDE + 3, cols), :] = mid_ref[near + begin + row, :, lanes].astype(F32)
            for col in range(3):
                for at, ref in ((col, left_ref), (cols + 3 + col, right_ref)):
                    edge = ref[col, pl.ds(near, 16), lanes].astype(F32)
                    slab[pl.ds(at, 3, stride=WIDE), :] = edge[begin:begin + 3]
            out_ref[:, lanes] = slab[pl.ds(0, 3 * WIDE), :].astype(BF16)


def rims(mid, left, right):
    chans = mid.shape[2]
    shape = jax.ShapeDtypeStruct((3 * WIDE, chans), BF16)
    return pl.pallas_call(
        rims_kernel,
        out_shape=(shape, shape),
        in_specs=[VMEM] * 3,
        out_specs=(VMEM, VMEM),
        scratch_shapes=[pltpu.VMEM((11 * WIDE, LANES), F32)],
        compiler_params=PARAMS,
    )(mid, left, right)


def conv_kernel(
    order_ref, mid_ref, low_ref, high_ref, left_ref, right_ref, taps_ref, bias_ref, gain_ref, shift_ref,
    out_ref, slab, taps, total,
):
    rows, cols, chans = mid_ref.shape
    block = 16
    taps[pl.ds(0, 49), :] = taps_ref[...].astype(F32)

    def chunk_step(chunk, carry):
        lanes = pl.ds(pl.multiple_of(chunk * LANES, LANES), LANES)
        slab[pl.ds(0, 3 * WIDE), :] = low_ref[:, lanes].astype(F32)
        slab[pl.ds((rows + 3) * WIDE, 3 * WIDE), :] = high_ref[:, lanes].astype(F32)
        for row in range(rows):
            slab[pl.ds((row + 3) * WIDE + 3, cols), :] = mid_ref[row, :, lanes].astype(F32)
        for col in range(3):
            slab[pl.ds(3 * WIDE + col, rows, stride=WIDE), :] = left_ref[col, :, lanes].astype(F32)
            slab[pl.ds(3 * WIDE + cols + 3 + col, rows, stride=WIDE), :] = right_ref[col, :, lanes].astype(F32)
        for base in range(0, rows, block):
            start = jnp.broadcast_to(bias_ref[:, lanes], (cols, LANES))
            sums = [start] * block
            for b in range(7):
                weights = [jnp.broadcast_to(taps[pl.ds(7 * a + b, 1), lanes], (cols, LANES)) for a in range(7)]
                for row in range(block + 6):
                    window = slab[pl.ds((base + row) * WIDE + b, cols), :]
                    for a in range(7):
                        if 0 <= row - a < block:
                            sums[row - a] = sums[row - a] + window * weights[a]
            for row in range(block):
                total[pl.ds((base + row) * cols, cols), lanes] = sums[row]
        return carry

    lax.fori_loop(0, chans // LANES, chunk_step, 0)

    step = 64
    for base in range(0, rows * cols, step):
        part = pl.ds(base, step)
        values = total[part, :]
        centre = jnp.mean(values, axis=-1, keepdims=True)
        values = values - centre
        spread = jnp.mean(values * values, axis=-1, keepdims=True)
        total[part, :] = values * lax.rsqrt(spread + 1e-06)
    for place in range(chans // LANES):
        lanes = pl.ds(pl.multiple_of(order_ref[place] * LANES, LANES), LANES)
        out_ref[:, pl.ds(place * LANES, LANES)] = (
            total[:, lanes] * gain_ref[:, lanes] + shift_ref[:, lanes]
        ).astype(BF16)


def conv_norm(order, mid, low, high, left, right, taps, bias, gain, offset):
    rows, cols, chans = mid.shape
    return pl.pallas_call(
        conv_kernel,
        out_shape=jax.ShapeDtypeStruct((rows * cols, chans), BF16),
        in_specs=[SMEM] + [VMEM] * 9,
        out_specs=VMEM,
        scratch_shapes=[
            pltpu.VMEM(((rows + 6) * WIDE, LANES), F32),
            pltpu.VMEM((56, chans), F32),
            pltpu.VMEM((rows * cols, chans), F32),
        ],
        compiler_params=PARAMS,
        cost_estimate=pl.CostEstimate(flops=100 * rows * cols * chans, bytes_accessed=2 << 20, transcendentals=0),
    )(order, mid, low, high, left, right, taps, bias, gain, offset)


def fill(weight, shards, spans):
    at = 0
    for shard, (start, count) in zip(shards, spans):
        weight[pl.ds(at, count), :] = shard[pl.ds(start, count), :]
        at += count


def begin_kernel(parts, spans, *refs):
    pixels, shards, bias_ref = refs[:parts], refs[parts:-parts - 2], refs[-parts - 2]
    outs, weight = refs[-parts - 1:-1], refs[-1]
    fill(weight, shards, spans)
    depth, hidden = weight.shape
    for pixel, out in zip(pixels, outs):
        for n in range(0, hidden, 256):
            cols = pl.ds(n, 256)
            out[:, cols] = (
                jnp.dot(pixel[:, pl.ds(0, depth)], weight[:, cols], preferred_element_type=F32) + bias_ref[:, cols]
            )


def begin(pixels, shards, bias):
    arrays, spans = [s[0] for s in shards], tuple(s[1:] for s in shards)
    depth = sum(count for _, count in spans)
    hidden = arrays[0].shape[1]
    outs = tuple(jax.ShapeDtypeStruct((p.shape[0], hidden), F32) for p in pixels)
    return pl.pallas_call(
        functools.partial(begin_kernel, len(pixels), spans),
        out_shape=outs,
        in_specs=[VMEM] * (len(pixels) + len(shards) + 1),
        out_specs=tuple(VMEM for _ in outs),
        scratch_shapes=[pltpu.VMEM((depth, hidden), BF16)],
        compiler_params=PARAMS,
        cost_estimate=pl.CostEstimate(
            flops=2 * depth * hidden * sum(p.shape[0] for p in pixels), bytes_accessed=1 << 20, transcendentals=0
        ),
    )(*pixels, *arrays, bias)


def up_kernel(parts, spans, *refs):
    pixels, sums, shards = refs[:parts], refs[parts:2 * parts], refs[2 * parts:-parts - 1]
    outs, weight = refs[-parts - 1:-1], refs[-1]
    fill(weight, shards, spans)
    depth, hidden = weight.shape
    for pixel, held, out in zip(pixels, sums, outs):
        rest = pl.ds(pixel.shape[1] - depth, depth)
        for n in range(0, hidden, 256):
            cols = pl.ds(n, 256)
            pre = held[:, cols] + jnp.dot(pixel[:, rest], weight[:, cols], preferred_element_type=F32)
            out[:, cols] = (0.5 * pre * (1.0 + lax.erf(pre * 0.7071067811865476))).astype(BF16)


def up(pixels, sums, shards):
    arrays, spans = [s[0] for s in shards], tuple(s[1:] for s in shards)
    depth = sum(count for _, count in spans)
    hidden = arrays[0].shape[1]
    outs = tuple(jax.ShapeDtypeStruct((p.shape[0], hidden), BF16) for p in pixels)
    return pl.pallas_call(
        functools.partial(up_kernel, len(pixels), spans),
        out_shape=outs,
        in_specs=[VMEM] * (2 * len(pixels) + len(shards)),
        out_specs=tuple(VMEM for _ in outs),
        scratch_shapes=[pltpu.VMEM((depth, hidden), BF16)],
        compiler_params=PARAMS,
        cost_estimate=pl.CostEstimate(
            flops=2 * depth * hidden * sum(p.shape[0] for p in pixels), bytes_accessed=1 << 20, transcendentals=0
        ),
    )(*pixels, *sums, *arrays)


def down_kernel(parts, spans, *refs):
    hidden, shards, outs = refs[:parts], refs[parts:-parts], refs[-parts:]
    for act, out in zip(hidden, outs):
        at = 0
        for shard, (start, count) in zip(shards, spans):
            out[:, pl.ds(at, count)] = lax.dot_general(
                act[...], shard[pl.ds(start, count), :], (((1,), (1,)), ((), ())), preferred_element_type=F32
            ).astype(BF16)
            at += count


def down(hidden, shards):
    arrays, spans = [s[0] for s in shards], tuple(s[1:] for s in shards)
    chans = sum(count for _, count in spans)
    outs = tuple(jax.ShapeDtypeStruct((h.shape[0], chans), BF16) for h in hidden)
    return pl.pallas_call(
        functools.partial(down_kernel, len(hidden), spans),
        out_shape=outs,
        in_specs=[VMEM] * (len(hidden) + len(shards)),
        out_specs=tuple(VMEM for _ in outs),
        compiler_params=PARAMS,
        cost_estimate=pl.CostEstimate(
            flops=2 * chans * hidden[0].shape[1] * sum(h.shape[0] for h in hidden), bytes_accessed=6 << 20,
            transcendentals=0,
        ),
    )(*hidden, *arrays)


def add_kernel(one_ref, two_ref, out_ref):
    out_ref[...] = (one_ref[...].astype(F32) + two_ref[...].astype(F32)).astype(BF16)


def add(one, two):
    return pl.pallas_call(
        add_kernel,
        out_shape=jax.ShapeDtypeStruct(one.shape, BF16),
        in_specs=[VMEM, VMEM],
        out_specs=VMEM,
        compiler_params=PARAMS,
    )(one, two)


def settle_kernel(first, order_ref, feature_ref, one_ref, two_ref, far_ref, bias_ref, scale_ref, *refs):
    out_ref, held, sems = refs[-3:]
    rows, chans = far_ref.shape
    copies = []
    for index in range(chans // LANES):
        lanes = pl.ds(pl.multiple_of(order_ref[first + index] * LANES, LANES), LANES)
        place = pl.ds(index * LANES, LANES)
        branch = (one_ref[:, place].astype(F32) + two_ref[:, place].astype(F32)) + far_ref[:, place].astype(F32)
        held[:, place] = (
            feature_ref[:, lanes].astype(F32) + scale_ref[:, lanes] * (branch + bias_ref[:, lanes])
        ).astype(BF16)
        copies.append(pltpu.make_async_copy(held.at[:, place], out_ref.at[:, lanes], sems.at[index]))
        copies[-1].start()
    for copy in copies:
        copy.wait()


def finish(order, features, groups, bias, scale):
    out, first = None, 0
    for one, two, far in groups:
        chans = far.shape[1]
        operands = (order, features, one, two, far, bias, scale)
        specs = [SMEM] + [VMEM] * 6
        if out is not None:
            operands, specs = operands + (out,), specs + [pl.BlockSpec(memory_space=pltpu.HBM)]
        out = pl.pallas_call(
            functools.partial(settle_kernel, first),
            out_shape=jax.ShapeDtypeStruct(features.shape, BF16),
            in_specs=specs,
            out_specs=pl.BlockSpec(memory_space=pltpu.HBM),
            scratch_shapes=[pltpu.VMEM(far.shape, BF16), pltpu.SemaphoreType.DMA((chans // LANES,))],
            input_output_aliases={7: 0} if out is not None else {},
            compiler_params=PARAMS,
        )(*operands)
        first += chans // LANES
    return out


def after(value, *earlier):
    return lax.optimization_barrier((value,) + earlier)[0]


STEPS = (0, 1, 3, 2)


def chunk_order(weight):
    count = lax.axis_size("lon")
    if weight.shape[0] != LANES:
        return jnp.arange(count * weight.shape[0] // LANES, dtype=jnp.int32)
    me = lax.axis_index("lon").astype(jnp.int32)
    group, side = me // 2, me % 2
    return jnp.stack(
        [((group - step) % (count // 2)) * 2 + (side ^ flip) for step in STEPS for flip in range(2)]
    ).astype(jnp.int32)


def local(
    features,
    depth_kernel,
    depth_bias,
    norm_gain,
    norm_bias,
    up_weight,
    up_bias,
    down_weight,
    down_bias,
    layer_scale,
):
    rows, cols, chans = features.shape
    lats, lons = lax.axis_size("lat"), lax.axis_size("lon")
    line = lambda v: v.reshape(1, -1)

    forward = [(i, i + 1) for i in range(lats - 1)]
    order = chunk_order(up_weight)
    conv_args = (depth_kernel.reshape(49, chans), line(depth_bias), line(norm_gain), line(norm_bias))
    z_of = lambda w, k: shift(w, "lon", k, 2)
    x_of = lambda w: swap(w, "lon", 1)
    if up_weight.shape[0] == LANES:
        both = jnp.concatenate([up_weight, down_weight], axis=0)
        first, last = edges(features)
        left = lax.ppermute(last, "lon", [(i, (i + 1) % lons) for i in range(lons)])
        right = lax.ppermute(first, "lon", [((i + 1) % lons, i) for i in range(lons)])
        top, bottom = rims(features, left, right)
        low = lax.ppermute(bottom, "lat", forward)
        high = lax.ppermute(top, "lat", [(b, a) for a, b in forward])
        uz1 = z_of(up_weight, 1)
        x0 = x_of(after(both, left))
        z3 = z_of(after(both, first), 3)
        uz2 = z_of(after(uz1, low), 1)
        ux1 = x_of(after(uz1, high))
        ux2 = x_of(after(uz2, x0))
        dz1 = z_of(jnp.concatenate([after(down_weight, uz2), x0[LANES:]], axis=0), 1)
        dz2 = z_of(dz1, 1)
        normed = conv_norm(order, features, after(low, top), high, left, right, *conv_args)
        x3 = x_of(after(z3, normed))
        across = swap(normed, "lat", 2)
        beside = swap(after(normed, ux1, uz2, x0), "lat", 1)
        opposite = swap(after(across, beside, x3), "lat", 1)
        up_shards = [(up_weight, 0, LANES), (x0, 0, LANES), (uz1, 0, LANES), (ux1, 0, LANES), (z3, 0, LANES), (x3, 0, LANES), (uz2, 0, LANES), (ux2, 0, LANES)]
        sums = begin([after(opposite, dz1), across, beside, normed], up_shards[:-1], line(up_bias))
        hid_opposite, hid_across, hid_beside, hid_own = up([opposite, across, beside, normed], sums, up_shards[-1:])
        down_a = [(down_weight, 0, LANES), (x0, LANES, LANES), (dz1, 0, 2 * LANES), (z3, LANES, LANES), (x3, LANES, LANES)]
        far_opp_a, = down([hid_opposite], down_a)
        far_acr_a, = down([hid_across], down_a)
        far_in_a = swap(far_opp_a, "lat", 1)
        far_a = add(far_acr_a, far_in_a)
        arrived_a = swap(far_a, "lat", 2)
        near_bes_a, = down([hid_beside], down_a)
        near_in_a = swap(near_bes_a, "lat", 1)
        near_own_a, = down([hid_own], down_a)
        down_b = [(dz2, 0, 2 * LANES)]
        far_opp_b, = down([hid_opposite], down_b)
        far_acr_b, = down([hid_across], down_b)
        far_in_b = swap(far_opp_b, "lat", 1)
        far_b = add(after(far_acr_b, far_a), far_in_b)
        arrived_b = swap(after(far_b, far_opp_a), "lat", 2)
        near_bes_b, = down([hid_beside], down_b)
        near_in_b = swap(near_bes_b, "lat", 1)
        near_own_b, = down([hid_own], down_b)
        groups = [(near_own_a, near_in_a, arrived_a), (near_own_b, near_in_b, arrived_b)]
    else:
        up_whole = lax.all_gather(up_weight, "lon", axis=0, tiled=True)
        up_shards = [(up_whole, 0, chans - LANES), (up_whole, chans - LANES, LANES)]
        down_a = [(lax.all_gather(down_weight, "lon", axis=0, tiled=True), 0, chans)]
        first, last = edges(features)
        left = lax.ppermute(last, "lon", [(i, (i + 1) % lons) for i in range(lons)])
        right = lax.ppermute(first, "lon", [((i + 1) % lons, i) for i in range(lons)])
        top, bottom = rims(features, left, right)
        low = lax.ppermute(bottom, "lat", forward)
        high = lax.ppermute(top, "lat", [(b, a) for a, b in forward])
        normed = conv_norm(order, features, low, high, left, right, *conv_args)
        across = swap(normed, "lat", 2)
        beside = swap(normed, "lat", 1)
        opposite = swap(across, "lat", 1)
        sums = begin([opposite, across, beside, normed], up_shards[:-1], line(up_bias))
        hid_opposite, hid_across, hid_beside, hid_own = up([opposite, across, beside, normed], sums, up_shards[-1:])
        far_opp_a, = down([hid_opposite], down_a)
        far_acr_a, = down([hid_across], down_a)
        far_in_a = swap(far_opp_a, "lat", 1)
        far_a = add(far_acr_a, far_in_a)
        arrived_a = swap(far_a, "lat", 2)
        near_bes_a, = down([hid_beside], down_a)
        near_in_a = swap(near_bes_a, "lat", 1)
        near_own_a, = down([hid_own], down_a)
        groups = [(near_own_a, near_in_a, arrived_a)]
    updated = finish(order, features.reshape(rows * cols, chans), groups, line(down_bias), line(layer_scale))
    return updated.reshape(rows, cols, chans)


def solution(mesh):
    placed = (
        P("lat", "lon", None),
        P(),
        P(),
        P(),
        P(),
        P("lon", "lat"),
        P("lat"),
        P("lon", "lat"),
        P(),
        P(),
    )
    return jax.shard_map(
        local, mesh=mesh, in_specs=placed, out_specs=P("lat", "lon", None), check_vma=False
    )
```

```python
import functools

import jax
import jax.numpy as jnp
from jax import lax
from jax.experimental import pallas as pl
from jax.experimental.pallas import tpu as pltpu
from jax.sharding import PartitionSpec as P

F32 = jnp.float32
BF16 = jnp.bfloat16
LANES = 128
VMEM = pl.BlockSpec(memory_space=pltpu.VMEM)
SMEM = pl.BlockSpec(memory_space=pltpu.SMEM)
PARAMS = pltpu.CompilerParams(vmem_limit_bytes=40 * 1024 * 1024)


def shift(value, axis, step, inner):
    count = lax.axis_size(axis)
    return lax.ppermute(value, axis, [(i, (i + step * inner) % count) for i in range(count)])


def swap(value, axis, bit):
    count = lax.axis_size(axis)
    return lax.ppermute(value, axis, [(i, i ^ bit) for i in range(count)])


def edges_kernel(mid_ref, first_ref, last_ref, slab):
    rows, cols, chans = mid_ref.shape
    for at in range(0, chans, LANES):
        lanes = pl.ds(at, LANES)
        slab[pl.ds(0, rows * cols), :] = mid_ref[:, :, lanes].astype(F32).reshape(rows * cols, LANES)
        for col in range(3):
            first_ref[col, :, lanes] = slab[pl.ds(col, rows, stride=cols), :].astype(BF16)
            last_ref[col, :, lanes] = slab[pl.ds(cols - 3 + col, rows, stride=cols), :].astype(BF16)


def edges(mid):
    rows, cols, chans = mid.shape
    block = 256
    shape = jax.ShapeDtypeStruct((3, rows, chans), BF16)
    out = pl.BlockSpec((3, rows, block), lambda i: (0, 0, i))
    return pl.pallas_call(
        edges_kernel,
        grid=(chans // block,),
        out_shape=(shape, shape),
        in_specs=[pl.BlockSpec((rows, cols, block), lambda i: (0, 0, i))],
        out_specs=(out, out),
        scratch_shapes=[pltpu.VMEM(((rows + 1) * cols, LANES), F32)],
        compiler_params=PARAMS,
    )(mid)


WIDE = 16


def rims_kernel(mid_ref, left_ref, right_ref, top_ref, bottom_ref, slab):
    rows, cols, chans = mid_ref.shape
    slab[...] = jnp.zeros_like(slab)

    @pl.loop(0, chans // LANES)
    def _(chunk):
        lanes = pl.ds(pl.multiple_of(chunk * LANES, LANES), LANES)
        for out_ref, near, begin in ((top_ref, 0, 0), (bottom_ref, rows - 16, 13)):
            for row in range(3):
                slab[pl.ds(row * WIDE + 3, cols), :] = mid_ref[near + begin + row, :, lanes].astype(F32)
            for col in range(3):
                for at, ref in ((col, left_ref), (cols + 3 + col, right_ref)):
                    edge = ref[col, pl.ds(near, 16), lanes].astype(F32)
                    slab[pl.ds(at, 3, stride=WIDE), :] = edge[begin:begin + 3]
            out_ref[:, lanes] = slab[pl.ds(0, 3 * WIDE), :].astype(BF16)


def rims(mid, left, right):
    chans = mid.shape[2]
    shape = jax.ShapeDtypeStruct((3 * WIDE, chans), BF16)
    return pl.pallas_call(
        rims_kernel,
        out_shape=(shape, shape),
        in_specs=[VMEM] * 3,
        out_specs=(VMEM, VMEM),
        scratch_shapes=[pltpu.VMEM((11 * WIDE, LANES), F32)],
        compiler_params=PARAMS,
    )(mid, left, right)


def conv_kernel(
    order_ref, mid_ref, low_ref, high_ref, left_ref, right_ref, taps_ref, bias_ref, gain_ref, shift_ref,
    out_ref, slab, taps, total,
):
    rows, cols, chans = mid_ref.shape
    block = 16
    taps[pl.ds(0, 49), :] = taps_ref[...].astype(F32)

    def chunk_step(chunk, carry):
        lanes = pl.ds(pl.multiple_of(chunk * LANES, LANES), LANES)
        slab[pl.ds(0, 3 * WIDE), :] = low_ref[:, lanes].astype(F32)
        slab[pl.ds((rows + 3) * WIDE, 3 * WIDE), :] = high_ref[:, lanes].astype(F32)
        for row in range(rows):
            slab[pl.ds((row + 3) * WIDE + 3, cols), :] = mid_ref[row, :, lanes].astype(F32)
        for col in range(3):
            slab[pl.ds(3 * WIDE + col, rows, stride=WIDE), :] = left_ref[col, :, lanes].astype(F32)
            slab[pl.ds(3 * WIDE + cols + 3 + col, rows, stride=WIDE), :] = right_ref[col, :, lanes].astype(F32)
        for base in range(0, rows, block):
            start = jnp.broadcast_to(bias_ref[:, lanes], (cols, LANES))
            sums = [start] * block
            for b in range(7):
                weights = [jnp.broadcast_to(taps[pl.ds(7 * a + b, 1), lanes], (cols, LANES)) for a in range(7)]
                for row in range(block + 6):
                    window = slab[pl.ds((base + row) * WIDE + b, cols), :]
                    for a in range(7):
                        if 0 <= row - a < block:
                            sums[row - a] = sums[row - a] + window * weights[a]
            for row in range(block):
                total[pl.ds((base + row) * cols, cols), lanes] = sums[row]
        return carry

    lax.fori_loop(0, chans // LANES, chunk_step, 0)

    step = 64
    for base in range(0, rows * cols, step):
        part = pl.ds(base, step)
        values = total[part, :]
        centre = jnp.mean(values, axis=-1, keepdims=True)
        values = values - centre
        spread = jnp.mean(values * values, axis=-1, keepdims=True)
        total[part, :] = values * lax.rsqrt(spread + 1e-06)
    for place in range(chans // LANES):
        lanes = pl.ds(pl.multiple_of(order_ref[place] * LANES, LANES), LANES)
        out_ref[:, pl.ds(place * LANES, LANES)] = (
            total[:, lanes] * gain_ref[:, lanes] + shift_ref[:, lanes]
        ).astype(BF16)


def conv_norm(order, mid, low, high, left, right, taps, bias, gain, offset):
    rows, cols, chans = mid.shape
    return pl.pallas_call(
        conv_kernel,
        out_shape=jax.ShapeDtypeStruct((rows * cols, chans), BF16),
        in_specs=[SMEM] + [VMEM] * 9,
        out_specs=VMEM,
        scratch_shapes=[
            pltpu.VMEM(((rows + 6) * WIDE, LANES), F32),
            pltpu.VMEM((56, chans), F32),
            pltpu.VMEM((rows * cols, chans), F32),
        ],
        compiler_params=PARAMS,
        cost_estimate=pl.CostEstimate(flops=100 * rows * cols * chans, bytes_accessed=2 << 20, transcendentals=0),
    )(order, mid, low, high, left, right, taps, bias, gain, offset)


def fill(weight, shards, spans):
    at = 0
    for shard, (start, count) in zip(shards, spans):
        weight[pl.ds(at, count), :] = shard[pl.ds(start, count), :]
        at += count


def begin_kernel(parts, spans, *refs):
    pixels, shards, bias_ref = refs[:parts], refs[parts:-parts - 2], refs[-parts - 2]
    outs, weight = refs[-parts - 1:-1], refs[-1]
    fill(weight, shards, spans)
    depth, hidden = weight.shape
    for pixel, out in zip(pixels, outs):
        for n in range(0, hidden, 256):
            cols = pl.ds(n, 256)
            out[:, cols] = (
                jnp.dot(pixel[:, pl.ds(0, depth)], weight[:, cols], preferred_element_type=F32) + bias_ref[:, cols]
            )


def begin(pixels, shards, bias):
    arrays, spans = [s[0] for s in shards], tuple(s[1:] for s in shards)
    depth = sum(count for _, count in spans)
    hidden = arrays[0].shape[1]
    outs = tuple(jax.ShapeDtypeStruct((p.shape[0], hidden), F32) for p in pixels)
    return pl.pallas_call(
        functools.partial(begin_kernel, len(pixels), spans),
        out_shape=outs,
        in_specs=[VMEM] * (len(pixels) + len(shards) + 1),
        out_specs=tuple(VMEM for _ in outs),
        scratch_shapes=[pltpu.VMEM((depth, hidden), BF16)],
        compiler_params=PARAMS,
        cost_estimate=pl.CostEstimate(
            flops=2 * depth * hidden * sum(p.shape[0] for p in pixels), bytes_accessed=1 << 20, transcendentals=0
        ),
    )(*pixels, *arrays, bias)


def up_kernel(parts, spans, *refs):
    pixels, sums, shards = refs[:parts], refs[parts:2 * parts], refs[2 * parts:-parts - 1]
    outs, weight = refs[-parts - 1:-1], refs[-1]
    fill(weight, shards, spans)
    depth, hidden = weight.shape
    for pixel, held, out in zip(pixels, sums, outs):
        rest = pl.ds(pixel.shape[1] - depth, depth)
        for n in range(0, hidden, 256):
            cols = pl.ds(n, 256)
            pre = held[:, cols] + jnp.dot(pixel[:, rest], weight[:, cols], preferred_element_type=F32)
            out[:, cols] = (0.5 * pre * (1.0 + lax.erf(pre * 0.7071067811865476))).astype(BF16)


def up(pixels, sums, shards):
    arrays, spans = [s[0] for s in shards], tuple(s[1:] for s in shards)
    depth = sum(count for _, count in spans)
    hidden = arrays[0].shape[1]
    outs = tuple(jax.ShapeDtypeStruct((p.shape[0], hidden), BF16) for p in pixels)
    return pl.pallas_call(
        functools.partial(up_kernel, len(pixels), spans),
        out_shape=outs,
        in_specs=[VMEM] * (2 * len(pixels) + len(shards)),
        out_specs=tuple(VMEM for _ in outs),
        scratch_shapes=[pltpu.VMEM((depth, hidden), BF16)],
        compiler_params=PARAMS,
        cost_estimate=pl.CostEstimate(
            flops=2 * depth * hidden * sum(p.shape[0] for p in pixels), bytes_accessed=1 << 20, transcendentals=0
        ),
    )(*pixels, *sums, *arrays)


def down_kernel(parts, spans, *refs):
    hidden, shards, outs = refs[:parts], refs[parts:-parts], refs[-parts:]
    for act, out in zip(hidden, outs):
        at = 0
        for shard, (start, count) in zip(shards, spans):
            out[:, pl.ds(at, count)] = lax.dot_general(
                act[...], shard[pl.ds(start, count), :], (((1,), (1,)), ((), ())), preferred_element_type=F32
            ).astype(BF16)
            at += count


def down(hidden, shards):
    arrays, spans = [s[0] for s in shards], tuple(s[1:] for s in shards)
    chans = sum(count for _, count in spans)
    outs = tuple(jax.ShapeDtypeStruct((h.shape[0], chans), BF16) for h in hidden)
    return pl.pallas_call(
        functools.partial(down_kernel, len(hidden), spans),
        out_shape=outs,
        in_specs=[VMEM] * (len(hidden) + len(shards)),
        out_specs=tuple(VMEM for _ in outs),
        compiler_params=PARAMS,
        cost_estimate=pl.CostEstimate(
            flops=2 * chans * hidden[0].shape[1] * sum(h.shape[0] for h in hidden), bytes_accessed=6 << 20,
            transcendentals=0,
        ),
    )(*hidden, *arrays)


def add_kernel(one_ref, two_ref, out_ref):
    out_ref[...] = (one_ref[...].astype(F32) + two_ref[...].astype(F32)).astype(BF16)


def add(one, two):
    return pl.pallas_call(
        add_kernel,
        out_shape=jax.ShapeDtypeStruct(one.shape, BF16),
        in_specs=[VMEM, VMEM],
        out_specs=VMEM,
        compiler_params=PARAMS,
    )(one, two)


def settle_kernel(first, order_ref, feature_ref, one_ref, two_ref, far_ref, bias_ref, scale_ref, *refs):
    out_ref, held, sems = refs[-3:]
    rows, chans = far_ref.shape
    copies = []
    for index in range(chans // LANES):
        lanes = pl.ds(pl.multiple_of(order_ref[first + index] * LANES, LANES), LANES)
        place = pl.ds(index * LANES, LANES)
        branch = (one_ref[:, place].astype(F32) + two_ref[:, place].astype(F32)) + far_ref[:, place].astype(F32)
        held[:, place] = (
            feature_ref[:, lanes].astype(F32) + scale_ref[:, lanes] * (branch + bias_ref[:, lanes])
        ).astype(BF16)
        copies.append(pltpu.make_async_copy(held.at[:, place], out_ref.at[:, lanes], sems.at[index]))
        copies[-1].start()
    for copy in copies:
        copy.wait()


def finish(order, features, groups, bias, scale):
    out, first = None, 0
    for one, two, far in groups:
        chans = far.shape[1]
        operands = (order, features, one, two, far, bias, scale)
        specs = [SMEM] + [VMEM] * 6
        if out is not None:
            operands, specs = operands + (out,), specs + [pl.BlockSpec(memory_space=pltpu.HBM)]
        out = pl.pallas_call(
            functools.partial(settle_kernel, first),
            out_shape=jax.ShapeDtypeStruct(features.shape, BF16),
            in_specs=specs,
            out_specs=pl.BlockSpec(memory_space=pltpu.HBM),
            scratch_shapes=[pltpu.VMEM(far.shape, BF16), pltpu.SemaphoreType.DMA((chans // LANES,))],
            input_output_aliases={7: 0} if out is not None else {},
            compiler_params=PARAMS,
        )(*operands)
        first += chans // LANES
    return out


def after(value, *earlier):
    return lax.optimization_barrier((value,) + earlier)[0]


STEPS = (0, 1, 3, 2)


def chunk_order(weight):
    count = lax.axis_size("lon")
    if weight.shape[0] != LANES:
        return jnp.arange(count * weight.shape[0] // LANES, dtype=jnp.int32)
    me = lax.axis_index("lon").astype(jnp.int32)
    group, side = me // 2, me % 2
    return jnp.stack(
        [((group - step) % (count // 2)) * 2 + (side ^ flip) for step in STEPS for flip in range(2)]
    ).astype(jnp.int32)


def local(
    features,
    depth_kernel,
    depth_bias,
    norm_gain,
    norm_bias,
    up_weight,
    up_bias,
    down_weight,
    down_bias,
    layer_scale,
):
    rows, cols, chans = features.shape
    lats, lons = lax.axis_size("lat"), lax.axis_size("lon")
    line = lambda v: v.reshape(1, -1)

    forward = [(i, i + 1) for i in range(lats - 1)]
    order = chunk_order(up_weight)
    conv_args = (depth_kernel.reshape(49, chans), line(depth_bias), line(norm_gain), line(norm_bias))
    z_of = lambda w, k: shift(w, "lon", k, 2)
    x_of = lambda w: swap(w, "lon", 1)
    if up_weight.shape[0] == LANES:
        both = jnp.concatenate([up_weight, down_weight], axis=0)
        first, last = edges(features)
        left = lax.ppermute(last, "lon", [(i, (i + 1) % lons) for i in range(lons)])
        right = lax.ppermute(first, "lon", [((i + 1) % lons, i) for i in range(lons)])
        top, bottom = rims(features, left, right)
        low = lax.ppermute(bottom, "lat", forward)
        high = lax.ppermute(top, "lat", [(b, a) for a, b in forward])
        uz1 = z_of(up_weight, 1)
        x0 = x_of(after(both, left))
        z3 = z_of(after(both, first), 3)
        uz2 = z_of(after(uz1, low), 1)
        ux1 = x_of(after(uz1, high))
        ux2 = x_of(after(uz2, x0))
        dz1 = z_of(jnp.concatenate([after(down_weight, uz2), x0[LANES:]], axis=0), 1)
        dz2 = z_of(dz1, 1)
        normed = conv_norm(order, features, after(low, top), high, left, right, *conv_args)
        x3 = x_of(after(z3, normed))
        across = swap(normed, "lat", 2)
        beside = swap(after(normed, ux1, uz2, x0), "lat", 1)
        opposite = swap(after(across, beside, x3), "lat", 1)
        up_shards = [(up_weight, 0, LANES), (x0, 0, LANES), (uz1, 0, LANES), (ux1, 0, LANES), (z3, 0, LANES), (x3, 0, LANES), (uz2, 0, LANES), (ux2, 0, LANES)]
        sums = begin([after(opposite, dz1), across, beside, normed], up_shards[:-1], line(up_bias))
        hid_opposite, hid_across, hid_beside, hid_own = up([opposite, across, beside, normed], sums, up_shards[-1:])
        down_a = [(down_weight, 0, LANES), (x0, LANES, LANES), (dz1, 0, 2 * LANES), (z3, LANES, LANES), (x3, LANES, LANES)]
        far_opp_a, = down([hid_opposite], down_a)
        far_acr_a, = down([hid_across], down_a)
        far_in_a = swap(far_opp_a, "lat", 1)
        far_a = add(far_acr_a, far_in_a)
        arrived_a = swap(far_a, "lat", 2)
        near_bes_a, = down([hid_beside], down_a)
        near_in_a = swap(near_bes_a, "lat", 1)
        down_b = [(dz2, 0, 2 * LANES)]
        far_opp_b, = down([hid_opposite], down_b)
        far_acr_b, = down([hid_across], down_b)
        far_in_b = swap(far_opp_b, "lat", 1)
        far_b = add(after(far_acr_b, far_a), far_in_b)
        near_own_a, = down([after(hid_own, far_b)], down_a)
        arrived_b = swap(after(far_b, far_opp_a), "lat", 2)
        near_bes_b, = down([after(hid_beside, far_b)], down_b)
        near_in_b = swap(near_bes_b, "lat", 1)
        near_own_b, = down([hid_own], down_b)
        groups = [(near_own_a, near_in_a, arrived_a), (near_own_b, near_in_b, arrived_b)]
    else:
        up_whole = lax.all_gather(up_weight, "lon", axis=0, tiled=True)
        up_shards = [(up_whole, 0, chans - LANES), (up_whole, chans - LANES, LANES)]
        down_a = [(lax.all_gather(down_weight, "lon", axis=0, tiled=True), 0, chans)]
        first, last = edges(features)
        left = lax.ppermute(last, "lon", [(i, (i + 1) % lons) for i in range(lons)])
        right = lax.ppermute(first, "lon", [((i + 1) % lons, i) for i in range(lons)])
        top, bottom = rims(features, left, right)
        low = lax.ppermute(bottom, "lat", forward)
        high = lax.ppermute(top, "lat", [(b, a) for a, b in forward])
        normed = conv_norm(order, features, low, high, left, right, *conv_args)
        across = swap(normed, "lat", 2)
        beside = swap(normed, "lat", 1)
        opposite = swap(across, "lat", 1)
        sums = begin([opposite, across, beside, normed], up_shards[:-1], line(up_bias))
        hid_opposite, hid_across, hid_beside, hid_own = up([opposite, across, beside, normed], sums, up_shards[-1:])
        far_opp_a, = down([hid_opposite], down_a)
        far_acr_a, = down([hid_across], down_a)
        far_in_a = swap(far_opp_a, "lat", 1)
        far_a = add(far_acr_a, far_in_a)
        arrived_a = swap(far_a, "lat", 2)
        near_bes_a, = down([hid_beside], down_a)
        near_in_a = swap(near_bes_a, "lat", 1)
        near_own_a, = down([hid_own], down_a)
        groups = [(near_own_a, near_in_a, arrived_a)]
    updated = finish(order, features.reshape(rows * cols, chans), groups, line(down_bias), line(layer_scale))
    return updated.reshape(rows, cols, chans)


def solution(mesh):
    placed = (
        P("lat", "lon", None),
        P(),
        P(),
        P(),
        P(),
        P("lon", "lat"),
        P("lat"),
        P("lon", "lat"),
        P(),
        P(),
    )
    return jax.shard_map(
        local, mesh=mesh, in_specs=placed, out_specs=P("lat", "lon", None), check_vma=False
    )
```
